256 devices in a mesh: dp: 16 (over y, x), vocab: 16 (over z, core).
Axes of the slice: x: 4, y: 4, z: 8, core: 2. Of those that a mesh axis runs over, the one named last changes fastest.
Arguments:
- hidden: bfloat16 [768, 4096], P(('dp', 'vocab')), may hold values from -240 to 240
- head_weight: bfloat16 [4096, 163840], P(None, ('dp', 'vocab')), may hold values from -0.40625 to 0.40625
- targets: int32 [768], P(('dp', 'vocab')), may hold values from 0 to 163839, as said below
- image_mask: int32 [768], P(('dp', 'vocab')), may hold values from 0 to 1
- lengths: int32 [16], replicated, may hold values from 12 to 48, as said below
- ref_logps: float32 [16], replicated, may hold values from -18 to -13
- pairing: int32 [16], replicated, may hold values from 0 to 15, each once
Outputs:
- grad_hidden: bfloat16 [768, 4096], P(('dp', 'vocab'))
- grad_head: bfloat16 [4096, 163840], P(None, ('dp', 'vocab'))
- mean_loss: float32 [], replicated
The draws below stay inside these ranges and needn't reach their ends.
Inputs may be any that keep to these rules, and one draw needn't show every extreme that they name: `targets`: each token's target lies in its modality's columns: at least 131072 where image_mask is 1, below it where image_mask is 0. `lengths`: some window is full.
All inputs are finite; a program needn't handle non-finite values.
Results may differ from the reference program's by a relative error of at most 0.0067.
Values may be sent and summed in bfloat16 or wider, within the bound.
No kernel may reach another device: no remote copies, remote signals or barrier semaphores. Data moves between devices by JAX's collectives and lax.ppermute only.
A program may use at most 128 MiB of HBM per device.

```python
import jax
import jax.numpy as jnp

D = 4096
V = 163840
CODES = 32768
WIN = 48
GROUPS = 16
TOKENS = 768


def token_tables(key):
    image_key = jax.random.fold_in(key, 11)
    text_key = jax.random.fold_in(key, 12)
    code_key = jax.random.fold_in(key, 13)
    image_flags = (jax.random.randint(image_key, (TOKENS,), 0, 3) == 0).astype(jnp.int32)
    text_ids = jax.random.randint(text_key, (TOKENS,), 0, V - CODES)
    code_ids = jax.random.randint(code_key, (TOKENS,), V - CODES, V)
    return (image_flags, jnp.where(image_flags == 1, code_ids, text_ids).astype(jnp.int32))


def draw_targets(key, part):
    return token_tables(key)[1]


def draw_image_mask(key, part):
    return token_tables(key)[0]


def draw_lengths(key, part):
    raw_lengths = jax.random.randint(jax.random.fold_in(key, 31), (GROUPS,), WIN // 4, WIN + 1)
    order = jax.random.permutation(jax.random.fold_in(key, 32), GROUPS)
    full_slot = jnp.arange(GROUPS, dtype=jnp.int32) == order[0]
    return jnp.where(full_slot, WIN, raw_lengths).astype(jnp.int32)


def draw_hidden(key, part):
    values = jnp.clip(jax.random.normal(jax.random.fold_in(key, 21), (TOKENS, D), jnp.float32), -6.0, 6.0)
    return values.astype(jnp.bfloat16)


def draw_head_weight(key, part):
    column_scale = 3.0 * D ** (-0.5)
    noise = jnp.clip(jax.random.normal(jax.random.fold_in(key, 41), (D, V), jnp.float32), -4.0, 4.0)
    offset = jnp.clip(jax.random.normal(jax.random.fold_in(key, 42), (D, 1), jnp.float32), -3.0, 3.0)
    values = column_scale * noise + 1.5 * column_scale * offset
    return values.astype(jnp.bfloat16)


def setup_inputs(seed: int = 0) -> dict:
    key_of = jax.random.split(jax.random.key(seed), 8)
    hidden = draw_hidden(jax.random.fold_in(key_of[7], 71), 0)
    head_weight = draw_head_weight(jax.random.fold_in(key_of[7], 71), 0)
    targets = draw_targets(jax.random.fold_in(key_of[7], 71), 0)
    image_mask = draw_image_mask(jax.random.fold_in(key_of[7], 71), 0)
    lengths = draw_lengths(jax.random.fold_in(key_of[7], 71), 0)
    ref_logps = jnp.clip(jax.random.uniform(key_of[5], (GROUPS,), jnp.float32, -18.0, -13.0), -18.0, -13.0)
    pairing = jax.random.permutation(key_of[6], GROUPS).astype(jnp.int32)
    return {"hidden": hidden, "head_weight": head_weight, "targets": targets, "image_mask": image_mask, "lengths": lengths, "ref_logps": ref_logps, "pairing": pairing}


NEG = -1e30
BETA = 1.0
LOSS_SCALE = 4096.0


def preference(token_lp, lengths, ref_logps, pairing):
    groups = lengths.shape[0]
    per_group = token_lp.reshape(groups, WIN)
    is_valid = jnp.arange(WIN, dtype=jnp.int32)[None, :] < lengths[:, None]
    token_count = lengths.astype(jnp.float32)
    policy = jnp.sum(jnp.where(is_valid, per_group, 0.0), axis=1) / token_count
    shifted = policy - ref_logps
    members = jnp.arange(groups, dtype=jnp.int32)
    chosen = (pairing[0::2][:, None] == members[None, :]).astype(jnp.float32)
    rejected = (pairing[1::2][:, None] == members[None, :]).astype(jnp.float32)
    pair_signs = chosen - rejected
    margin = BETA * jnp.sum(pair_signs * shifted[None, :], axis=1)
    mean_loss = jnp.mean(jax.nn.softplus(-margin))
    pair_weight = -LOSS_SCALE * BETA * jax.nn.sigmoid(-margin) / margin.shape[0]
    group_weight = jnp.sum(pair_weight[:, None] * pair_signs, axis=0) / token_count
    token_weight = jnp.where(is_valid, group_weight[:, None], 0.0).reshape(-1)
    return mean_loss, token_weight


def reference(hidden, head_weight, targets, image_mask, lengths, ref_logps, pairing):
    logits = jnp.dot(hidden, head_weight, preferred_element_type=jnp.float32)
    column_ids = jnp.arange(V, dtype=jnp.int32)
    code_column = column_ids >= V - CODES
    in_range = (image_mask[:, None] == 1) == code_column[None, :]
    masked = jnp.where(in_range, logits, NEG)
    row_peak = jnp.max(masked, axis=1)
    row_total = jnp.sum(jnp.where(in_range, jnp.exp(masked - row_peak[:, None]), 0.0), axis=1)
    log_norm = row_peak + jnp.log(row_total)
    is_target = column_ids[None, :] == targets[:, None]
    target_logit = jnp.sum(jnp.where(is_target, logits, 0.0), axis=1)
    token_lp = target_logit - log_norm
    mean_loss, token_weight = preference(token_lp, lengths, ref_logps, pairing)
    row_probs = jnp.where(in_range, jnp.exp(logits - log_norm[:, None]), 0.0)
    logit_grad = (token_weight[:, None] * (is_target.astype(jnp.float32) - row_probs)).astype(jnp.bfloat16)
    grad_hidden = jnp.dot(logit_grad, head_weight.T, preferred_element_type=jnp.float32).astype(jnp.bfloat16)
    grad_head = jnp.dot(hidden.T, logit_grad, preferred_element_type=jnp.float32).astype(jnp.bfloat16)
    return grad_hidden, grad_head, mean_loss
```

```python
import functools

import jax
import jax.numpy as jnp
from jax import lax
from jax.experimental import pallas as pl
from jax.experimental.pallas import tpu as pltpu
from jax.sharding import Mesh, PartitionSpec as P

V = 163840
CODES = 32768
WIN = 48
NEG = -1e30
BETA = 1.0
LOSS_SCALE = 4096.0

D = 4096
HALF = D // 2
COLS = 640
TOKENS = 768
META = 128
WIDE = HALF + META
NY, NX, NZ, NC = 4, 4, 8, 2
AXES = ("y", "x", "z", "c")
OFF = (0, 1, 3, 2)
bf16 = jnp.bfloat16
f32 = jnp.float32
VMEM = pl.BlockSpec(memory_space=pltpu.VMEM)
SMEM = pl.BlockSpec(memory_space=pltpu.SMEM)
MB = 1024 * 1024


def flat(y, x, z, c):
    return ((y % NY * NX + x % NX) * NZ + z % NZ) * NC + c


def fetch(value, source):
    pairs = [
        (flat(*source(y, x, z, c)), flat(y, x, z, c))
        for y in range(NY) for x in range(NX) for z in range(NZ) for c in range(NC)
    ]
    return lax.ppermute(value, AXES, pairs)


def middle(step):
    return lambda y, x, z, c: (y + step, x, z, c) if c == 0 else (y, x + step, z, c)


def final(step):
    return lambda y, x, z, c: (y, x + step, z, c) if c == 0 else (y + step, x, z, c)


def along_z(step):
    return lambda y, x, z, c: (y, x, z + step, c)


def along_y(step):
    return lambda y, x, z, c: (y + step, x, z, c)


def along_x(step):
    return lambda y, x, z, c: (y, x + step, z, c)


def near(q):
    return lambda y, x, z, c: (y, x, z ^ (q >> 1), c ^ (q & 1))


def window(ids, core, s, k):
    y, x = ids[0], ids[1]
    across = core == 0
    last = (jnp.where(across, x, y) + OFF[s]) % 4
    mid = (jnp.where(across, y, x) + OFF[k]) % 4
    return jnp.where(across, mid * NX + last, last * NX + mid)


def place(ids, s, q):
    zz, low = ids[2] // 2, ids[2] % 2 * 2 + ids[3]
    return (zz + OFF[s]) % 4 * 4 + (low ^ q)


def call(kernel, outs, ins, scratch=(), vmem=48, **cost):
    return pl.pallas_call(
        kernel,
        out_shape=outs,
        in_specs=ins,
        out_specs=jax.tree.map(lambda _: VMEM, outs),
        scratch_shapes=list(scratch),
        compiler_params=pltpu.CompilerParams(vmem_limit_bytes=vmem * MB),
        cost_estimate=pl.CostEstimate(
            flops=cost.get("flops", 0), bytes_accessed=cost.get("bytes_accessed", 0), transcendentals=0
        ),
    )


def shape(dims, dtype):
    return jax.ShapeDtypeStruct(dims, dtype)


def join_window_kernel(ids, u0, u1, u2, u3, out, tok, meta):
    for s, u in enumerate((u0, u1, u2, u3)):
        for q in range(4):
            dev = place(ids, s, q)
            tok[pl.ds(pl.multiple_of(dev * 48, 16), 48), :] = u[q, 0:48, :].astype(f32)
            meta[pl.ds(pl.multiple_of(dev * 16, 16), 16), :] = u[q, 48:64, :].astype(f32)
    for j in range(3):
        for r in range(16):
            out[j * 16:(j + 1) * 16, r * 128:(r + 1) * 128] = tok[pl.ds(j * 16 + r, 16, stride=48), :].astype(bf16)
        out[j * 16:(j + 1) * 16, HALF:WIDE] = meta[pl.ds(j, 16, stride=16), :].astype(bf16)


def join_window(ids, parts):
    return call(
        join_window_kernel,
        shape((WIN, WIDE), bf16),
        [SMEM] + [VMEM] * 4,
        [pltpu.VMEM((768, 128), f32), pltpu.VMEM((256, 128), f32)],
    )(ids, *parts)


def columns_of(rows):
    full = jnp.concatenate([rows, jnp.zeros((128 - rows.shape[0], 128), f32)], axis=0)
    return full.T


def logits_kernel(ids, a0, a1, a2, a3, b0, b1, b2, b3, head, hidden, logits, stats, target, meta, cols):
    core = ids[3]
    own = pl.multiple_of(core * HALF, HALF)
    oth = pl.multiple_of((1 - core) * HALF, HALF)
    for s, (a, b) in enumerate(((a0, b0), (a1, b1), (a2, b2), (a3, b3))):
        for k in range(4):
            row = pl.multiple_of(window(ids, core, s, k) * WIN, 16)
            hidden[pl.ds(row, WIN), pl.ds(own, HALF)] = a[k, :, 0:HALF]
            meta[pl.ds(row, WIN), :] = a[k, :, HALF:WIDE].astype(f32)
            row = pl.multiple_of(window(ids, 1 - core, s, k) * WIN, 16)
            hidden[pl.ds(row, WIN), pl.ds(oth, HALF)] = b[k, :, 0:HALF]
    first = ids[4] * COLS
    rows = 256
    column = first + lax.broadcasted_iota(jnp.int32, (rows, COLS), 1)
    lane = lax.broadcasted_iota(jnp.int32, (rows, 128), 1)
    for i in range(TOKENS // rows):
        at = pl.ds(i * rows, rows)
        part = jnp.dot(hidden[at, :], head[...], preferred_element_type=f32)
        logits[at, :] = part
        digits = meta[at, :]
        goal = (digits[:, 0:1] + 256.0 * digits[:, 1:2] + 65536.0 * digits[:, 2:3]).astype(jnp.int32)
        in_range = (goal >= V - CODES) == (column >= V - CODES)
        masked = jnp.where(in_range, part, NEG)
        peak = jnp.max(masked, axis=1, keepdims=True)
        total = jnp.sum(jnp.where(in_range, jnp.exp(masked - peak), 0.0), axis=1, keepdims=True)
        hit = jnp.sum(jnp.where(column == goal, part, 0.0), axis=1, keepdims=True)
        cols[at, :] = jnp.where(
            lane == 0, peak, jnp.where(lane == 1, total, jnp.where(lane == 2, hit, goal.astype(f32)))
        )
    stats[...] = jnp.zeros_like(stats)
    target[...] = jnp.zeros_like(target)
    for b in range(TOKENS // 128):
        turned = cols[b * 128:(b + 1) * 128, :].T
        for i in range(3):
            stats[i, b:b + 1, :] = turned[i:i + 1, :]
        target[b:b + 1, :] = turned[3:4, :]


def local_logits(ids, own, other, head):
    return call(
        logits_kernel,
        (
            shape((TOKENS, D), bf16),
            shape((TOKENS, COLS), f32),
            shape((3, 8, 128), f32),
            shape((8, 128), f32),
        ),
        [SMEM] + [VMEM] * 9,
        [pltpu.VMEM((TOKENS, 128), f32), pltpu.VMEM((TOKENS, 128), f32)],
        flops=2 * TOKENS * D * COLS,
        bytes_accessed=25 * MB,
    )(ids, *own, *other, head)


def merge_kernel(a, b, c, d, out):
    peak = jnp.maximum(jnp.maximum(a[0], b[0]), jnp.maximum(c[0], d[0]))
    term = [v[1] * jnp.exp(v[0] - peak) for v in (a, b, c, d)]
    out[0] = peak
    out[1] = (term[0] + term[1]) + (term[2] + term[3])
    out[2] = (a[2] + b[2]) + (c[2] + d[2])


def merge(a, b, c, d):
    return call(merge_kernel, shape((3, 8, 128), f32), [VMEM] * 4)(a, b, c, d)


def preference(stats, lengths, ref_logps, pairing):
    rows = lax.broadcasted_iota(jnp.int32, (1, TOKENS), 1)
    inner = rows % WIN
    position = inner % 16 * 3 + inner // 16
    log_norm = stats[0] + jnp.log(jnp.maximum(stats[1], 1e-37))
    token_lp = (stats[2] - log_norm)[:6].reshape(1, TOKENS)
    groups = lengths.shape[0]
    members = jnp.arange(groups, dtype=jnp.int32)
    is_valid = (rows // WIN == members[:, None]) & (position < lengths[:, None])
    token_count = lengths.astype(f32)
    policy = jnp.sum(jnp.where(is_valid, token_lp, 0.0), axis=1) / token_count
    shifted = policy - ref_logps
    chosen = (pairing[0::2][:, None] == members[None, :]).astype(f32)
    rejected = (pairing[1::2][:, None] == members[None, :]).astype(f32)
    pair_signs = chosen - rejected
    margin = BETA * jnp.sum(pair_signs * shifted[None, :], axis=1)
    mean_loss = jnp.mean(jax.nn.softplus(-margin))
    pair_weight = -LOSS_SCALE * BETA * jax.nn.sigmoid(-margin) / margin.shape[0]
    group_weight = jnp.sum(pair_weight[:, None] * pair_signs, axis=0) / token_count
    token_weight = jnp.sum(jnp.where(is_valid, group_weight[:, None], 0.0), axis=0)
    weight = jnp.pad(token_weight.reshape(6, 128), ((0, 2), (0, 0)))
    return mean_loss, log_norm, weight


BLOCK = 512


def grad_kernel(ids, logits, norm, weight, target, head, grad, out):
    @pl.when(pl.program_id(0) == 0)
    def _():
        norm_c, weight_c, goal_c = columns_of(norm[...]), columns_of(weight[...]), columns_of(target[...])
        column = ids[4] * COLS + lax.broadcasted_iota(jnp.int32, (128, COLS), 1)
        for b in range(TOKENS // 128):
            goal = goal_c[:, b:b + 1].astype(jnp.int32)
            in_range = (goal >= V - CODES) == (column >= V - CODES)
            at = slice(b * 128, (b + 1) * 128)
            prob = jnp.exp(jnp.where(in_range, logits[at, :] - norm_c[:, b:b + 1], NEG))
            grad[at, :] = (weight_c[:, b:b + 1] * ((column == goal).astype(f32) - prob)).astype(bf16)

    out[...] = lax.dot_general(
        grad[...], head[...], (((1,), (1,)), ((), ())), preferred_element_type=f32
    ).astype(out.dtype)


def grad_other(ids, logits, norm, weight, target, head):
    return pl.pallas_call(
        grad_kernel,
        grid_spec=pltpu.PrefetchScalarGridSpec(
            num_scalar_prefetch=1,
            grid=(HALF // BLOCK,),
            in_specs=[
                pl.BlockSpec((TOKENS, COLS), lambda i, ids: (0, 0)),
                pl.BlockSpec((8, 128), lambda i, ids: (0, 0)),
                pl.BlockSpec((8, 128), lambda i, ids: (0, 0)),
                pl.BlockSpec((8, 128), lambda i, ids: (0, 0)),
                pl.BlockSpec((BLOCK, COLS), lambda i, ids: ((1 - ids[3]) * (HALF // BLOCK) + i, 0)),
            ],
            out_specs=[
                pl.BlockSpec((TOKENS, COLS), lambda i, ids: (0, 0)),
                pl.BlockSpec((TOKENS, BLOCK), lambda i, ids: (0, i)),
            ],
        ),
        out_shape=(shape((TOKENS, COLS), bf16), shape((TOKENS, HALF), bf16)),
        compiler_params=pltpu.CompilerParams(vmem_limit_bytes=40 * MB),
        cost_estimate=pl.CostEstimate(flops=TOKENS * D * COLS, bytes_accessed=9 * MB, transcendentals=0),
    )(ids, logits, norm, weight, target, head)


def grad_own_kernel(ids, grad, head, out):
    out[...] = lax.dot_general(
        grad[...], head[...], (((1,), (1,)), ((), ())), preferred_element_type=f32
    ).astype(out.dtype)


def grad_own(ids, grad, head):
    return pl.pallas_call(
        grad_own_kernel,
        grid_spec=pltpu.PrefetchScalarGridSpec(
            num_scalar_prefetch=1,
            grid=(HALF // BLOCK,),
            in_specs=[
                pl.BlockSpec((TOKENS, COLS), lambda i, ids: (0, 0)),
                pl.BlockSpec((BLOCK, COLS), lambda i, ids: (ids[3] * (HALF // BLOCK) + i, 0)),
            ],
            out_specs=pl.BlockSpec((TOKENS, BLOCK), lambda i, ids: (0, i)),
        ),
        out_shape=shape((TOKENS, HALF), f32),
        compiler_params=pltpu.CompilerParams(vmem_limit_bytes=40 * MB),
        cost_estimate=pl.CostEstimate(flops=TOKENS * D * COLS, bytes_accessed=10 * MB, transcendentals=0),
    )(ids, grad, head)


def head_kernel(hidden, grad, out):
    out[...] = lax.dot_general(
        hidden[...], grad[...], (((0,), (0,)), ((), ())), preferred_element_type=f32
    ).astype(out.dtype)


def grad_head_of(hidden, grad):
    return pl.pallas_call(
        head_kernel,
        grid=(D // BLOCK,),
        in_specs=[
            pl.BlockSpec((TOKENS, BLOCK), lambda i: (0, i)),
            pl.BlockSpec((TOKENS, COLS), lambda i: (0, 0)),
        ],
        out_specs=pl.BlockSpec((BLOCK, COLS), lambda i: (i, 0)),
        out_shape=shape((D, COLS), bf16),
        compiler_params=pltpu.CompilerParams(vmem_limit_bytes=40 * MB),
        cost_estimate=pl.CostEstimate(flops=2 * TOKENS * D * COLS, bytes_accessed=12 * MB, transcendentals=0),
    )(hidden, grad)


def split_final_kernel(order, own, other, r0, r1, r2, r3):
    total = own[...] + other[...].astype(f32)
    step = pl.program_id(0)
    for s, r in enumerate((r0, r1, r2, r3)):
        @pl.when(step // 4 == s)
        def _(r=r):
            r[0] = total.astype(r.dtype)


def split_final(order, own, other):
    block = pl.BlockSpec((WIN, HALF), lambda i, order: (order[i], 0))

    def out(s):
        return pl.BlockSpec((1, WIN, HALF), lambda i, order: (jnp.clip(i - 4 * s, 0, 3), 0, 0))

    return pl.pallas_call(
        split_final_kernel,
        grid_spec=pltpu.PrefetchScalarGridSpec(
            num_scalar_prefetch=1,
            grid=(16,),
            in_specs=[block, block],
            out_specs=[out(s) for s in range(4)],
        ),
        out_shape=[shape((4, WIN, HALF), f32 if s == 0 else bf16) for s in range(4)],
        cost_estimate=pl.CostEstimate(flops=0, bytes_accessed=14 * MB, transcendentals=0),
    )(order, own, other)


def add_four(a, b, c, d):
    return (a.astype(f32) + d.astype(f32)) + (b.astype(f32) + c.astype(f32))


def split_middle_kernel(a, b, c, d, q0, q1, q2, q3):
    for k, q in enumerate((q0, q1, q2, q3)):
        q[...] = add_four(a[k], b[k], c[k], d[k]).astype(q.dtype)


def split_middle(a, b, c, d):
    return call(
        split_middle_kernel,
        [shape((WIN, HALF), f32 if k == 0 else bf16) for k in range(4)],
        [VMEM] * 4,
        bytes_accessed=6 * MB,
    )(a, b, c, d)


def split_window_kernel(ids, a, b, c, d, u0, u1, u2, u3, tok):
    total = add_four(a[...], b[...], c[...], d[...])
    for j in range(3):
        for r in range(16):
            tok[pl.ds(j * 16 + r, 16, stride=48), :] = total[j * 16:(j + 1) * 16, r * 128:(r + 1) * 128]
    for s, u in enumerate((u0, u1, u2, u3)):
        for q in range(4):
            dev = place(ids, s, q)
            u[q] = tok[pl.ds(pl.multiple_of(dev * 48, 16), 48), :].astype(u.dtype)


def split_window(ids, a, b, c, d):
    return call(
        split_window_kernel,
        [shape((4, 48, 128), f32 if s == 0 else bf16) for s in range(4)],
        [SMEM] + [VMEM] * 4,
        [pltpu.VMEM((768, 128), f32)],
    )(ids, a, b, c, d)


def split_near_kernel(a, b, c, d, v0, v1, v2, v3):
    for q, v in enumerate((v0, v1, v2, v3)):
        v[...] = add_four(a[q], b[q], c[q], d[q]).astype(v.dtype)


def split_near(a, b, c, d):
    return call(
        split_near_kernel,
        [shape((48, 128), f32 if q == 0 else bf16) for q in range(4)],
        [VMEM] * 4,
    )(a, b, c, d)


def local(hidden, head_weight, targets, image_mask, lengths, ref_logps, pairing):
    y, x, z, c = (lax.axis_index(a) for a in AXES)
    ids = jnp.stack([y, x, z, c, flat(y, x, z, c)]).astype(jnp.int32)

    digits = jnp.stack([targets % 256, targets // 256 % 256, targets // 65536], axis=1)
    meta = jnp.pad(digits.astype(f32).astype(bf16), ((0, 13), (0, 125)))
    halves = hidden.reshape(3, 2, 16, 128)
    first, second = (jnp.concatenate([halves[:, i].reshape(48, 128), meta], axis=0) for i in range(2))
    mine = jnp.where(c == 0, first, second)
    theirs = jnp.where(c == 0, second, first)

    near_parts = jnp.stack(
        [mine, fetch(theirs, near(1)), fetch(mine, near(2)), fetch(theirs, near(3))]
    )
    z_parts = [near_parts] + [fetch(near_parts, along_z(2 * o)) for o in OFF[1:]]
    block = join_window(ids, z_parts)
    blocks = jnp.stack([block] + [fetch(block, middle(o)) for o in OFF[1:]])
    own = [blocks] + [fetch(blocks, final(o)) for o in OFF[1:]]
    other = [fetch(v, near(1)) for v in own]

    rows, logits, stats, target = local_logits(ids, own, other, head_weight)
    stats = merge(stats, *(fetch(stats, near(q)) for q in (1, 2, 3)))
    for ring in (lambda o: along_z(2 * o), along_y, along_x):
        stats = merge(stats, *(fetch(stats, ring(o)) for o in (2, 1, 3)))
    mean_loss, log_norm, weight = preference(stats, lengths, ref_logps, pairing)

    logit_grad, send = grad_other(ids, logits, log_norm, weight, target, head_weight)
    received = fetch(send, near(1))
    keep = grad_own(ids, logit_grad, head_weight)
    grad_head = grad_head_of(rows, logit_grad)

    order = jnp.stack([window(ids, c, s, k) for s in range(4) for k in range(4)]).astype(jnp.int32)
    parts = split_final(order, keep, received)
    parts = split_middle(parts[0], *(fetch(parts[s], final(-OFF[s])) for s in (1, 2, 3)))
    parts = split_window(ids, parts[0], *(fetch(parts[s], middle(-OFF[s])) for s in (1, 2, 3)))
    parts = split_near(parts[0], *(fetch(parts[s], along_z(-2 * OFF[s])) for s in (1, 2, 3)))
    far1, near2, far3 = (fetch(parts[q], near(q)) for q in (1, 2, 3))
    own_half = (parts[0] + near2.astype(f32)).astype(bf16).reshape(3, HALF)
    other_half = (far1.astype(f32) + far3.astype(f32)).astype(bf16).reshape(3, HALF)
    grad_hidden = jnp.where(
        c == 0,
        jnp.concatenate([own_half, other_half], axis=1),
        jnp.concatenate([other_half, own_half], axis=1),
    )
    return grad_hidden, grad_head, mean_loss


def solution(mesh):
    fine = Mesh(mesh.devices.reshape(NY, NX, NZ, NC), AXES)
    return jax.shard_map(
        local,
        mesh=fine,
        in_specs=(P(AXES, None), P(None, AXES), P(AXES), P(AXES), P(), P(), P()),
        out_specs=(P(AXES, None), P(None, AXES), P()),
        check_vma=False,
    )
```

```python
import functools

import jax
import jax.numpy as jnp
from jax import lax
from jax.experimental import pallas as pl
from jax.experimental.pallas import tpu as pltpu
from jax.sharding import Mesh, PartitionSpec as P

V = 163840
CODES = 32768
WIN = 48
NEG = -1e30
BETA = 1.0
LOSS_SCALE = 4096.0

D = 4096
HALF = D // 2
COLS = 640
TOKENS = 768
META = 128
WIDE = HALF + META
NY, NX, NZ, NC = 4, 4, 8, 2
AXES = ("y", "x", "z", "c")
OFF = (0, 1, 3, 2)
bf16 = jnp.bfloat16
f32 = jnp.float32
VMEM = pl.BlockSpec(memory_space=pltpu.VMEM)
SMEM = pl.BlockSpec(memory_space=pltpu.SMEM)
HBM = pl.BlockSpec(memory_space=pltpu.HBM)
MB = 1024 * 1024
PIECE = HALF // 2


def flat(y, x, z, c):
    return ((y % NY * NX + x % NX) * NZ + z % NZ) * NC + c


def fetch(value, source):
    pairs = [
        (flat(*source(y, x, z, c)), flat(y, x, z, c))
        for y in range(NY) for x in range(NX) for z in range(NZ) for c in range(NC)
    ]
    return lax.ppermute(value, AXES, pairs)


def middle(step):
    return lambda y, x, z, c: (y + step, x, z, c) if c == 0 else (y, x + step, z, c)


def final(step):
    return lambda y, x, z, c: (y, x + step, z, c) if c == 0 else (y + step, x, z, c)


def along_z(step):
    return lambda y, x, z, c: (y, x, z + step, c)


def along_y(step):
    return lambda y, x, z, c: (y + step, x, z, c)


def along_x(step):
    return lambda y, x, z, c: (y, x + step, z, c)


def near(q):
    return lambda y, x, z, c: (y, x, z ^ (q >> 1), c ^ (q & 1))


def window(ids, core, s, k):
    y, x = ids[0], ids[1]
    across = core == 0
    last = (jnp.where(across, x, y) + OFF[s]) % 4
    mid = (jnp.where(across, y, x) + OFF[k]) % 4
    return jnp.where(across, mid * NX + last, last * NX + mid)


def place(ids, s, q):
    zz, low = ids[2] // 2, ids[2] % 2 * 2 + ids[3]
    return (zz + OFF[s]) % 4 * 4 + (low ^ q)


def call(kernel, outs, ins, scratch=(), vmem=10, **cost):
    return pl.pallas_call(
        kernel,
        out_shape=outs,
        in_specs=ins,
        out_specs=jax.tree.map(lambda _: VMEM, outs),
        scratch_shapes=list(scratch),
        compiler_params=pltpu.CompilerParams(vmem_limit_bytes=vmem * MB),
        cost_estimate=pl.CostEstimate(
            flops=cost.get("flops", 0), bytes_accessed=cost.get("bytes_accessed", 0), transcendentals=0
        ),
    )


def shape(dims, dtype):
    return jax.ShapeDtypeStruct(dims, dtype)


def join_window_kernel(ids, u0, u1, u2, u3, out, tok, meta):
    for s, u in enumerate((u0, u1, u2, u3)):
        for q in range(4):
            dev = place(ids, s, q)
            tok[pl.ds(pl.multiple_of(dev * 48, 16), 48), :] = u[q, 0:48, :].astype(f32)
            meta[pl.ds(pl.multiple_of(dev * 16, 16), 16), :] = u[q, 48:64, :].astype(f32)
    for j in range(3):
        for r in range(16):
            out[j * 16:(j + 1) * 16, r * 128:(r + 1) * 128] = tok[pl.ds(j * 16 + r, 16, stride=48), :].astype(bf16)
        out[j * 16:(j + 1) * 16, HALF:WIDE] = meta[pl.ds(j, 16, stride=16), :].astype(bf16)


def join_window(ids, parts):
    return call(
        join_window_kernel,
        shape((WIN, WIDE), bf16),
        [SMEM] + [VMEM] * 4,
        [pltpu.VMEM((768, 128), f32), pltpu.VMEM((256, 128), f32)],
    )(ids, *parts)


def join_blocks_kernel(a, b, c, d, out):
    for k, v in enumerate((a, b, c, d)):
        out[k] = v[...]


def join_blocks(*blocks):
    return call(join_blocks_kernel, shape((4, WIN, WIDE), bf16), [VMEM] * 4)(*blocks)


def gate_kernel(value, after, out):
    out[...] = value[...]


def gate(value, after):
    return pl.pallas_call(
        gate_kernel,
        out_shape=shape(value.shape, value.dtype),
        in_specs=[VMEM, VMEM],
        out_specs=VMEM,
        compiler_params=pltpu.CompilerParams(vmem_limit_bytes=10 * MB),
    )(value, after)


def columns_of(rows):
    full = jnp.concatenate([rows, jnp.zeros((128 - rows.shape[0], 128), f32)], axis=0)
    return full.T


def logits_kernel(
    ids, a0, a1, a2, a3, b0, b1, b2, b3, head_hbm, hidden_hbm, logits, stats, target, meta, cols, hidden, head, in_sem, out_sem
):
    rows = 256
    into = pltpu.make_async_copy(head_hbm, head, in_sem)
    into.start()
    core = ids[3]
    own = pl.multiple_of(core * HALF, HALF)
    oth = pl.multiple_of((1 - core) * HALF, HALF)
    for s, (a, b) in enumerate(((a0, b0), (a1, b1), (a2, b2), (a3, b3))):
        for k in range(4):
            row = pl.multiple_of(window(ids, core, s, k) * WIN, 16)
            hidden[pl.ds(row, WIN), pl.ds(own, HALF)] = a[k, :, 0:HALF]
            meta[pl.ds(row, WIN), :] = a[k, :, HALF:WIDE].astype(f32)
            row = pl.multiple_of(window(ids, 1 - core, s, k) * WIN, 16)
            hidden[pl.ds(row, WIN), pl.ds(oth, HALF)] = b[k, :, 0:HALF]
    out = pltpu.make_async_copy(hidden, hidden_hbm, out_sem)
    out.start()
    into.wait()
    first = ids[4] * COLS
    column = first + lax.broadcasted_iota(jnp.int32, (rows, COLS), 1)
    lane = lax.broadcasted_iota(jnp.int32, (rows, 128), 1)
    for i in range(TOKENS // rows):
        at = pl.ds(i * rows, rows)
        part = jnp.dot(hidden[at, :], head[...], preferred_element_type=f32)
        logits[at, :] = part
        digits = meta[at, :]
        goal = (digits[:, 0:1] + 256.0 * digits[:, 1:2] + 65536.0 * digits[:, 2:3]).astype(jnp.int32)
        in_range = (goal >= V - CODES) == (column >= V - CODES)
        masked = jnp.where(in_range, part, NEG)
        peak = jnp.max(masked, axis=1, keepdims=True)
        total = jnp.sum(jnp.where(in_range, jnp.exp(masked - peak), 0.0), axis=1, keepdims=True)
        hit = jnp.sum(jnp.where(column == goal, part, 0.0), axis=1, keepdims=True)
        cols[at, :] = jnp.where(
            lane == 0, peak, jnp.where(lane == 1, total, jnp.where(lane == 2, hit, goal.astype(f32)))
        )
    stats[...] = jnp.zeros_like(stats)
    target[...] = jnp.zeros_like(target)
    for b in range(TOKENS // 128):
        turned = cols[b * 128:(b + 1) * 128, :].T
        for i in range(3):
            stats[i, b:b + 1, :] = turned[i:i + 1, :]
        target[b:b + 1, :] = turned[3:4, :]
    out.wait()


def local_logits(ids, own, other, head):
    return pl.pallas_call(
        logits_kernel,
        out_shape=(
            shape((TOKENS, D), bf16),
            shape((TOKENS, COLS), f32),
            shape((3, 8, 128), f32),
            shape((8, 128), f32),
        ),
        in_specs=[SMEM] + [VMEM] * 8 + [HBM],
        out_specs=(HBM, VMEM, VMEM, VMEM),
        scratch_shapes=[
            pltpu.VMEM((TOKENS, 128), f32),
            pltpu.VMEM((TOKENS, 128), f32),
            pltpu.VMEM((TOKENS, D), bf16),
            pltpu.VMEM((D, COLS), bf16),
            pltpu.SemaphoreType.DMA,
            pltpu.SemaphoreType.DMA,
        ],
        compiler_params=pltpu.CompilerParams(vmem_limit_bytes=46 * MB),
        cost_estimate=pl.CostEstimate(flops=2 * TOKENS * D * COLS, bytes_accessed=20 * MB, transcendentals=0),
    )(ids, *own, *other, head)


def merge_kernel(a, b, c, d, out):
    peak = jnp.maximum(jnp.maximum(a[0], b[0]), jnp.maximum(c[0], d[0]))
    term = [v[1] * jnp.exp(v[0] - peak) for v in (a, b, c, d)]
    out[0] = peak
    out[1] = (term[0] + term[1]) + (term[2] + term[3])
    out[2] = (a[2] + b[2]) + (c[2] + d[2])


def merge(a, b, c, d):
    return call(merge_kernel, shape((3, 8, 128), f32), [VMEM] * 4)(a, b, c, d)


def preference(stats, lengths, ref_logps, pairing):
    rows = lax.broadcasted_iota(jnp.int32, (1, TOKENS), 1)
    inner = rows % WIN
    position = inner % 16 * 3 + inner // 16
    log_norm = stats[0] + jnp.log(jnp.maximum(stats[1], 1e-37))
    token_lp = (stats[2] - log_norm)[:6].reshape(1, TOKENS)
    groups = lengths.shape[0]
    members = jnp.arange(groups, dtype=jnp.int32)
    is_valid = (rows // WIN == members[:, None]) & (position < lengths[:, None])
    token_count = lengths.astype(f32)
    policy = jnp.sum(jnp.where(is_valid, token_lp, 0.0), axis=1) / token_count
    shifted = policy - ref_logps
    chosen = (pairing[0::2][:, None] == members[None, :]).astype(f32)
    rejected = (pairing[1::2][:, None] == members[None, :]).astype(f32)
    pair_signs = chosen - rejected
    margin = BETA * jnp.sum(pair_signs * shifted[None, :], axis=1)
    mean_loss = jnp.mean(jax.nn.softplus(-margin))
    pair_weight = -LOSS_SCALE * BETA * jax.nn.sigmoid(-margin) / margin.shape[0]
    group_weight = jnp.sum(pair_weight[:, None] * pair_signs, axis=0) / token_count
    token_weight = jnp.sum(jnp.where(is_valid, group_weight[:, None], 0.0), axis=0)
    weight = jnp.pad(token_weight.reshape(6, 128), ((0, 2), (0, 0)))
    return mean_loss, log_norm, weight


BLOCK = 512
STEP = 256


def load_head(half, piece, head, rows, sems):
    copies = []
    for i in range(PIECE // STEP):
        at = pl.multiple_of(half * HALF + piece * PIECE + i * STEP, STEP)
        copies.append(pltpu.make_async_copy(head.at[pl.ds(at, STEP), :], rows.at[i], sems.at[i]))
        copies[-1].start()
    return copies


def times_head(grad, rows):
    return lax.dot_general(grad, rows, (((1,), (1,)), ((), ())), preferred_element_type=f32)


HEAD_SCRATCH = [pltpu.VMEM((PIECE // STEP, STEP, COLS), bf16), pltpu.SemaphoreType.DMA((PIECE // STEP,))]


def other_piece(piece, ids, grad, head, out, rows, sems, prepare=None):
    copies = load_head(1 - ids[3], piece, head, rows, sems)
    if prepare is not None:
        prepare()
    for i, copy in enumerate(copies):
        copy.wait()
        out[:, i * STEP:(i + 1) * STEP] = times_head(grad[...], rows[i]).astype(out.dtype)


def grad_other_first_kernel(ids, logits, norm, weight, target, head, grad, out, rows, sems):
    def prepare():
        norm_c, weight_c, goal_c = columns_of(norm[...]), columns_of(weight[...]), columns_of(target[...])
        column = ids[4] * COLS + lax.broadcasted_iota(jnp.int32, (128, COLS), 1)
        for b in range(TOKENS // 128):
            goal = goal_c[:, b:b + 1].astype(jnp.int32)
            in_range = (goal >= V - CODES) == (column >= V - CODES)
            at = slice(b * 128, (b + 1) * 128)
            prob = jnp.exp(jnp.where(in_range, logits[at, :] - norm_c[:, b:b + 1], NEG))
            grad[at, :] = (weight_c[:, b:b + 1] * ((column == goal).astype(f32) - prob)).astype(bf16)

    other_piece(0, ids, grad, head, out, rows, sems, prepare)


def grad_other_first(ids, logits, norm, weight, target, head):
    return call(
        grad_other_first_kernel,
        (shape((TOKENS, COLS), bf16), shape((TOKENS, PIECE), bf16)),
        [SMEM] + [VMEM] * 4 + [HBM],
        HEAD_SCRATCH,
        vmem=48,
        flops=TOKENS * PIECE * COLS * 2,
        bytes_accessed=6 * MB,
    )(ids, logits, norm, weight, target, head)


def grad_other_second(ids, grad, head):
    return call(
        functools.partial(other_piece, 1),
        shape((TOKENS, PIECE), bf16),
        [SMEM, VMEM, HBM],
        HEAD_SCRATCH,
        vmem=48,
        flops=TOKENS * PIECE * COLS * 2,
        bytes_accessed=4 * MB,
    )(ids, grad, head)


def grad_own_kernel(piece, ids, grad, head, other, after, r0, r1, r2, r3, mark, rows, sems, total):
    copies = load_head(ids[3], piece, head, rows, sems)
    mark[...] = jnp.zeros_like(mark)
    for i, copy in enumerate(copies):
        copy.wait()
        at = slice(i * STEP, (i + 1) * STEP)
        total[...] = times_head(grad[...], rows[i]) + other[:, at].astype(f32)
        for s, r in enumerate((r0, r1, r2, r3)):
            for k in range(4):
                row = pl.multiple_of(window(ids, ids[3], s, k) * WIN, 16)
                r[k, :, at] = total[pl.ds(row, WIN), :].astype(r.dtype)


def grad_own(ids, grad, head, other, piece, after):
    return call(
        functools.partial(grad_own_kernel, piece),
        [shape((4, WIN, PIECE), f32 if s == 0 else bf16) for s in range(4)] + [shape((8, 128), f32)],
        [SMEM, VMEM, HBM, VMEM, VMEM],
        HEAD_SCRATCH + [pltpu.VMEM((TOKENS, STEP), f32)],
        vmem=46,
        flops=piece * 2 * TOKENS * PIECE * COLS,
        bytes_accessed=piece * 8 * MB,
    )(ids, grad, head, other, after)


def head_kernel(hidden, grad, after, out, mark):
    mark[...] = jnp.zeros_like(mark)
    out[...] = lax.dot_general(
        hidden[...], grad[...], (((0,), (0,)), ((), ())), preferred_element_type=f32
    ).astype(out.dtype)


def grad_head_of(hidden, grad, after):
    return pl.pallas_call(
        head_kernel,
        grid=(D // BLOCK,),
        in_specs=[
            pl.BlockSpec((TOKENS, BLOCK), lambda i: (0, i)),
            pl.BlockSpec((TOKENS, COLS), lambda i: (0, 0)),
            pl.BlockSpec((8, 128), lambda i: (0, 0)),
        ],
        out_specs=(pl.BlockSpec((BLOCK, COLS), lambda i: (i, 0)), pl.BlockSpec((8, 128), lambda i: (0, 0))),
        out_shape=(shape((D, COLS), bf16), shape((8, 128), f32)),
        compiler_params=pltpu.CompilerParams(vmem_limit_bytes=20 * MB),
        cost_estimate=pl.CostEstimate(flops=2 * TOKENS * D * COLS, bytes_accessed=12 * MB, transcendentals=0),
    )(hidden, grad, after)


def add_four(a, b, c, d):
    return (a.astype(f32) + d.astype(f32)) + (b.astype(f32) + c.astype(f32))


def split_middle_kernel(*refs):
    ins, outs = refs[:8], refs[9:]
    for k, q in enumerate(outs):
        for h in range(2):
            q[:, h * PIECE:(h + 1) * PIECE] = add_four(*(v[k] for v in ins[4 * h:4 * h + 4])).astype(q.dtype)


def split_middle(pieces, after):
    return call(
        split_middle_kernel,
        [shape((WIN, HALF), f32 if k == 0 else bf16) for k in range(4)],
        [VMEM] * 9,
        bytes_accessed=6 * MB,
    )(*pieces, after)


def split_window_kernel(ids, a, b, c, d, u0, u1, u2, u3, tok):
    total = add_four(a[...], b[...], c[...], d[...])
    for j in range(3):
        for r in range(16):
            tok[pl.ds(j * 16 + r, 16, stride=48), :] = total[j * 16:(j + 1) * 16, r * 128:(r + 1) * 128]
    for s, u in enumerate((u0, u1, u2, u3)):
        for q in range(4):
            dev = place(ids, s, q)
            u[q] = tok[pl.ds(pl.multiple_of(dev * 48, 16), 48), :].astype(u.dtype)


def split_window(ids, a, b, c, d):
    return call(
        split_window_kernel,
        [shape((4, 48, 128), f32)] * 4,
        [SMEM] + [VMEM] * 4,
        [pltpu.VMEM((768, 128), f32)],
    )(ids, a, b, c, d)


def split_near_kernel(a, b, c, d, v0, v1, v2, v3):
    for q, v in enumerate((v0, v1, v2, v3)):
        v[...] = add_four(a[q], b[q], c[q], d[q]).astype(v.dtype)


def split_near(a, b, c, d):
    return call(
        split_near_kernel,
        [shape((48, 128), f32)] * 4,
        [VMEM] * 4,
    )(a, b, c, d)


def local(hidden, head_weight, targets, image_mask, lengths, ref_logps, pairing):
    y, x, z, c = (lax.axis_index(a) for a in AXES)
    ids = jnp.stack([y, x, z, c, flat(y, x, z, c)]).astype(jnp.int32)

    digits = jnp.stack([targets % 256, targets // 256 % 256, targets // 65536], axis=1)
    meta = jnp.pad(digits.astype(f32).astype(bf16), ((0, 13), (0, 125)))
    halves = hidden.reshape(3, 2, 16, 128)
    first, second = (jnp.concatenate([halves[:, i].reshape(48, 128), meta], axis=0) for i in range(2))
    mine = jnp.where(c == 0, first, second)
    theirs = jnp.where(c == 0, second, first)

    near_parts = jnp.stack(
        [mine, fetch(theirs, near(1)), fetch(mine, near(2)), fetch(theirs, near(3))]
    )
    z_parts = [near_parts] + [fetch(near_parts, along_z(2 * o)) for o in OFF[1:]]
    block = join_window(ids, z_parts)
    blocks = join_blocks(block, *(fetch(block, middle(o)) for o in OFF[1:]))
    other = [fetch(blocks, near(1))]
    blocks = gate(blocks, other[0])
    own = [blocks] + [fetch(blocks, final(o)) for o in OFF[1:]]
    other = other + [fetch(v, near(1)) for v in own[1:]]

    rows, logits, stats, target = local_logits(ids, own, other, head_weight)
    stats = merge(stats, *(fetch(stats, near(q)) for q in (1, 2, 3)))
    for ring in (lambda o: along_z(2 * o), along_y, along_x):
        stats = merge(stats, *(fetch(stats, ring(o)) for o in (2, 1, 3)))
    mean_loss, log_norm, weight = preference(stats, lengths, ref_logps, pairing)

    logit_grad, send = grad_other_first(ids, logits, log_norm, weight, target, head_weight)
    received = [fetch(send, near(1))]
    received.append(fetch(grad_other_second(ids, logit_grad, head_weight), near(1)))
    pieces = []
    mark = weight
    for piece in range(2):
        *parts, mark = grad_own(ids, logit_grad, head_weight, received[piece], piece, mark)
        pieces += [parts[0]] + [fetch(parts[s], final(-OFF[s])) for s in (1, 2, 3)]
    grad_head, mark = grad_head_of(rows, logit_grad, mark)
    parts = split_middle(pieces, mark)
    parts = split_window(ids, parts[0], *(fetch(parts[s], middle(-OFF[s])) for s in (1, 2, 3)))
    parts = split_near(parts[0], *(fetch(parts[s], along_z(-2 * OFF[s])) for s in (1, 2, 3)))
    far1, near2, far3 = (fetch(parts[q], near(q)) for q in (1, 2, 3))
    own_half = (parts[0] + near2.astype(f32)).astype(bf16).reshape(3, HALF)
    other_half = (far1.astype(f32) + far3.astype(f32)).astype(bf16).reshape(3, HALF)
    grad_hidden = jnp.where(
        c == 0,
        jnp.concatenate([own_half, other_half], axis=1),
        jnp.concatenate([other_half, own_half], axis=1),
    )
    return grad_hidden, grad_head, mean_loss


def solution(mesh):
    fine = Mesh(mesh.devices.reshape(NY, NX, NZ, NC), AXES)
    return jax.shard_map(
        local,
        mesh=fine,
        in_specs=(P(AXES, None), P(None, AXES), P(AXES), P(AXES), P(), P(), P()),
        out_specs=(P(AXES, None), P(None, AXES), P()),
        check_vma=False,
    )
```

```python
import functools

import jax
import jax.numpy as jnp
from jax import lax
from jax.experimental import pallas as pl
from jax.experimental.pallas import tpu as pltpu
from jax.sharding import Mesh, PartitionSpec as P

V = 163840
CODES = 32768
WIN = 48
NEG = -1e30
BETA = 1.0
LOSS_SCALE = 4096.0

D = 4096
HALF = D // 2
COLS = 640
TOKENS = 768
META = 128
WIDE = HALF + META
NY, NX, NZ, NC = 4, 4, 8, 2
AXES = ("y", "x", "z", "c")
OFF = (0, 1, 3, 2)
bf16 = jnp.bfloat16
f32 = jnp.float32
VMEM = pl.BlockSpec(memory_space=pltpu.VMEM)
SMEM = pl.BlockSpec(memory_space=pltpu.SMEM)
HBM = pl.BlockSpec(memory_space=pltpu.HBM)
MB = 1024 * 1024
PIECE = HALF // 2


def flat(y, x, z, c):
    return ((y % NY * NX + x % NX) * NZ + z % NZ) * NC + c


def fetch(value, source):
    pairs = [
        (flat(*source(y, x, z, c)), flat(y, x, z, c))
        for y in range(NY) for x in range(NX) for z in range(NZ) for c in range(NC)
    ]
    return lax.ppermute(value, AXES, pairs)


def middle(step):
    return lambda y, x, z, c: (y + step, x, z, c) if c == 0 else (y, x + step, z, c)


def final(step):
    return lambda y, x, z, c: (y, x + step, z, c) if c == 0 else (y + step, x, z, c)


def near(q):
    return lambda y, x, z, c: (y, x, z ^ (q >> 1), c ^ (q & 1))


def window(ids, core, s, k):
    y, x = ids[0], ids[1]
    across = core == 0
    last = (jnp.where(across, x, y) + OFF[s]) % 4
    mid = (jnp.where(across, y, x) + OFF[k]) % 4
    return jnp.where(across, mid * NX + last, last * NX + mid)


def call(kernel, outs, ins, scratch=(), vmem=10, **cost):
    return pl.pallas_call(
        kernel,
        out_shape=outs,
        in_specs=ins,
        out_specs=jax.tree.map(lambda _: VMEM, outs),
        scratch_shapes=list(scratch),
        compiler_params=pltpu.CompilerParams(vmem_limit_bytes=vmem * MB),
        cost_estimate=pl.CostEstimate(
            flops=cost.get("flops", 0), bytes_accessed=cost.get("bytes_accessed", 0), transcendentals=0
        ),
    )


def shape(dims, dtype):
    return jax.ShapeDtypeStruct(dims, dtype)


def join_window_kernel(ids, parts, out, tok, meta):
    for dev in range(16):
        tok[dev * 48:(dev + 1) * 48, :] = parts[dev, 0:48, :].astype(f32)
        meta[dev * 16:(dev + 1) * 16, :] = parts[dev, 48:64, :].astype(f32)
    for j in range(3):
        for r in range(16):
            out[j * 16:(j + 1) * 16, r * 128:(r + 1) * 128] = tok[pl.ds(j * 16 + r, 16, stride=48), :].astype(bf16)
        out[j * 16:(j + 1) * 16, HALF:WIDE] = meta[pl.ds(j, 16, stride=16), :].astype(bf16)


def join_window(ids, parts):
    return call(
        join_window_kernel,
        shape((WIN, WIDE), bf16),
        [SMEM, VMEM],
        [pltpu.VMEM((768, 128), f32), pltpu.VMEM((256, 128), f32)],
    )(ids, parts)


def join_blocks_kernel(a, b, c, d, out):
    for k, v in enumerate((a, b, c, d)):
        out[k] = v[...]


def join_blocks(*blocks):
    return call(join_blocks_kernel, shape((4, WIN, WIDE), bf16), [VMEM] * 4)(*blocks)


def gate_kernel(value, first, second, out):
    out[...] = value[...]


def gate(value, first, second):
    return pl.pallas_call(
        gate_kernel,
        out_shape=shape(value.shape, value.dtype),
        in_specs=[VMEM] * 3,
        out_specs=VMEM,
        compiler_params=pltpu.CompilerParams(vmem_limit_bytes=10 * MB),
    )(value, first, second)


def columns_of(rows):
    full = jnp.concatenate([rows, jnp.zeros((128 - rows.shape[0], 128), f32)], axis=0)
    return full.T


def load_kernel(head_hbm, head, mark, sem):
    mark[...] = jnp.zeros_like(mark)
    copy = pltpu.make_async_copy(head_hbm, head, sem)
    copy.start()
    copy.wait()


def load_head(head):
    return call(
        load_kernel,
        (shape((D, COLS), bf16), shape((8, 128), f32)),
        [HBM],
        [pltpu.SemaphoreType.DMA],
        vmem=8,
        bytes_accessed=10 * MB,
    )(head)


def logits_kernel(
    ids, a0, a1, a2, a3, b0, b1, b2, b3, head, hidden, logits, stats, target, meta, cols
):
    rows = 256
    core = ids[3]
    own = pl.multiple_of(core * HALF, HALF)
    oth = pl.multiple_of((1 - core) * HALF, HALF)
    for s, (a, b) in enumerate(((a0, b0), (a1, b1), (a2, b2), (a3, b3))):
        for k in range(4):
            row = pl.multiple_of(window(ids, core, s, k) * WIN, 16)
            hidden[pl.ds(row, WIN), pl.ds(own, HALF)] = a[k, :, 0:HALF]
            meta[pl.ds(row, WIN), :] = a[k, :, HALF:WIDE].astype(f32)
            row = pl.multiple_of(window(ids, 1 - core, s, k) * WIN, 16)
            hidden[pl.ds(row, WIN), pl.ds(oth, HALF)] = b[k, :, 0:HALF]
    first = ids[4] * COLS
    column = first + lax.broadcasted_iota(jnp.int32, (rows, COLS), 1)
    lane = lax.broadcasted_iota(jnp.int32, (rows, 128), 1)
    for i in range(TOKENS // rows):
        at = pl.ds(i * rows, rows)
        part = jnp.dot(hidden[at, :], head[...], preferred_element_type=f32)
        logits[at, :] = part
        digits = meta[at, :]
        goal = (digits[:, 0:1] + 256.0 * digits[:, 1:2] + 65536.0 * digits[:, 2:3]).astype(jnp.int32)
        in_range = (goal >= V - CODES) == (column >= V - CODES)
        masked = jnp.where(in_range, part, NEG)
        peak = jnp.max(masked, axis=1, keepdims=True)
        total = jnp.sum(jnp.where(in_range, jnp.exp(masked - peak), 0.0), axis=1, keepdims=True)
        hit = jnp.sum(jnp.where(column == goal, part, 0.0), axis=1, keepdims=True)
        cols[at, :] = jnp.where(
            lane == 0, peak, jnp.where(lane == 1, total, jnp.where(lane == 2, hit, goal.astype(f32)))
        )
    stats[...] = jnp.zeros_like(stats)
    target[...] = jnp.zeros_like(target)
    for b in range(TOKENS // 128):
        turned = cols[b * 128:(b + 1) * 128, :].T
        for i in range(3):
            stats[i, b:b + 1, :] = turned[i:i + 1, :]
        target[b:b + 1, :] = turned[3:4, :]


def local_logits(ids, own, other, head):
    return pl.pallas_call(
        logits_kernel,
        out_shape=(
            shape((TOKENS, D), bf16),
            shape((TOKENS, COLS), f32),
            shape((3, 8, 128), f32),
            shape((8, 128), f32),
        ),
        in_specs=[SMEM] + [VMEM] * 9,
        out_specs=(VMEM, VMEM, VMEM, VMEM),
        scratch_shapes=[
            pltpu.VMEM((TOKENS, 128), f32),
            pltpu.VMEM((TOKENS, 128), f32),
        ],
        compiler_params=pltpu.CompilerParams(vmem_limit_bytes=25 * MB),
        cost_estimate=pl.CostEstimate(flops=2 * TOKENS * D * COLS, bytes_accessed=20 * MB, transcendentals=0),
    )(ids, *own, *other, head)


def exchange(value, axes):
    return lax.all_to_all(jnp.broadcast_to(value[None], (16,) + value.shape), axes, 0, 0, tiled=True)


def merged(parts):
    peak = parts[0, 0]
    for i in range(1, 16):
        peak = jnp.maximum(peak, parts[i, 0])
    total = jnp.zeros_like(peak)
    hit = jnp.zeros_like(peak)
    for i in range(16):
        total += parts[i, 1] * jnp.exp(parts[i, 0] - peak)
        hit += parts[i, 2]
    return peak, total, hit


def merge_kernel(parts, out):
    for i in range(16):
        out[i, 0], out[i, 1], out[i, 2] = merged(parts)


def merge(parts):
    return call(merge_kernel, shape((16, 3, 8, 128), f32), [VMEM])(parts)


def preference_kernel(parts, lengths, ref_logps, pairing, norm, weight, loss):
    peak, total, hit = merged(parts)
    log_norm = peak + jnp.log(jnp.maximum(total, 1e-37))
    token_lp = hit - log_norm
    rows = lax.broadcasted_iota(jnp.int32, (8, 128), 0) * 128 + lax.broadcasted_iota(jnp.int32, (8, 128), 1)
    inner = rows % WIN
    group, position = rows // WIN, inner % 16 * 3 + inner // 16
    pairs = pairing.shape[0] // 2
    token_weight = jnp.zeros((8, 128), f32)
    losses = jnp.zeros((1, 1), f32)
    for k in range(pairs):
        sides = []
        for g in (pairing[2 * k], pairing[2 * k + 1]):
            count = lengths[g].astype(f32)
            live = (group == g) & (position < lengths[g])
            policy = jnp.sum(jnp.where(live, token_lp, 0.0), keepdims=True) / count
            sides.append((live, count, policy - ref_logps[g]))
        (live_c, count_c, chosen), (live_r, count_r, rejected) = sides
        margin = BETA * (chosen - rejected)
        losses += jnp.maximum(-margin, 0.0) + jnp.log1p(jnp.exp(-jnp.abs(margin)))
        pair_weight = -LOSS_SCALE * BETA * jax.nn.sigmoid(-margin) / pairs
        token_weight += jnp.where(live_c, pair_weight / count_c, 0.0)
        token_weight -= jnp.where(live_r, pair_weight / count_r, 0.0)
    norm[...] = log_norm
    weight[...] = token_weight
    loss[...] = jnp.broadcast_to(losses / pairs, (8, 128))


def preference(parts, lengths, ref_logps, pairing):
    return call(
        preference_kernel,
        [shape((8, 128), f32)] * 3,
        [VMEM, SMEM, SMEM, SMEM],
    )(parts, lengths, ref_logps, pairing)


BLOCK = 512
STEP = 256


def times_head(grad, rows):
    return lax.dot_general(grad, rows, (((1,), (1,)), ((), ())), preferred_element_type=f32)


def head_rows(half, start):
    return pl.ds(pl.multiple_of(half * HALF + start, STEP), STEP)


def other_piece(piece, ids, grad, head, out):
    for i in range(PIECE // STEP):
        rows = head[head_rows(1 - ids[3], piece * PIECE + i * STEP), :]
        out[:, i * STEP:(i + 1) * STEP] = times_head(grad[...], rows).astype(out.dtype)


def grad_other_first_kernel(ids, logits, norm, weight, target, head, grad, out):
    norm_c, weight_c, goal_c = columns_of(norm[...]), columns_of(weight[...]), columns_of(target[...])
    column = ids[4] * COLS + lax.broadcasted_iota(jnp.int32, (128, COLS), 1)
    for b in range(TOKENS // 128):
        goal = goal_c[:, b:b + 1].astype(jnp.int32)
        in_range = (goal >= V - CODES) == (column >= V - CODES)
        at = slice(b * 128, (b + 1) * 128)
        prob = jnp.exp(jnp.where(in_range, logits[at, :] - norm_c[:, b:b + 1], NEG))
        grad[at, :] = (weight_c[:, b:b + 1] * ((column == goal).astype(f32) - prob)).astype(bf16)
    other_piece(0, ids, grad, head, out)


def grad_other_first(ids, logits, norm, weight, target, head):
    return call(
        grad_other_first_kernel,
        (shape((TOKENS, COLS), bf16), shape((TOKENS, PIECE), bf16)),
        [SMEM] + [VMEM] * 5,
        vmem=16,
        flops=TOKENS * PIECE * COLS * 2,
        bytes_accessed=6 * MB,
    )(ids, logits, norm, weight, target, head)


def grad_other_second(ids, grad, head):
    return call(
        functools.partial(other_piece, 1),
        shape((TOKENS, PIECE), bf16),
        [SMEM, VMEM, VMEM],
        vmem=16,
        flops=TOKENS * PIECE * COLS * 4,
        bytes_accessed=16 * MB,
    )(ids, grad, head)


def arrived_kernel(value, mark):
    mark[...] = jnp.zeros_like(mark)


def arrived(value):
    return call(arrived_kernel, shape((8, 128), f32), [VMEM], vmem=4)(value)


def grad_own_kernel(ids, grad, head, other0, other1, after, r0, r1, r2, r3, mark, total):
    mark[...] = jnp.zeros_like(mark)
    for i in range(HALF // STEP):
        at = slice(i * STEP, (i + 1) * STEP)
        other = (other0, other1)[i * STEP // PIECE]
        inner = i * STEP % PIECE
        total[...] = times_head(grad[...], head[head_rows(ids[3], i * STEP), :])
        total[...] += other[:, inner:inner + STEP].astype(f32)
        for s, r in enumerate((r0, r1, r2, r3)):
            for k in range(4):
                row = pl.multiple_of(window(ids, ids[3], s, k) * WIN, 16)
                r[k, :, at] = total[pl.ds(row, WIN), :].astype(r.dtype)


def grad_own(ids, grad, head, other, after):
    return call(
        grad_own_kernel,
        [shape((4, WIN, HALF), f32 if s == 0 else bf16) for s in range(4)] + [shape((8, 128), f32)],
        [SMEM] + [VMEM] * 5,
        [pltpu.VMEM((TOKENS, STEP), f32)],
        vmem=22,
    )(ids, grad, head, *other, after)


def head_kernel(hidden, grad, after, out, mark):
    mark[...] = jnp.zeros_like(mark)
    out[...] = lax.dot_general(
        hidden[...], grad[...], (((0,), (0,)), ((), ())), preferred_element_type=f32
    ).astype(out.dtype)


def grad_head_of(hidden, grad, after):
    return pl.pallas_call(
        head_kernel,
        grid=(D // BLOCK,),
        in_specs=[
            pl.BlockSpec((TOKENS, BLOCK), lambda i: (0, i)),
            pl.BlockSpec((TOKENS, COLS), lambda i: (0, 0)),
            pl.BlockSpec((8, 128), lambda i: (0, 0)),
        ],
        out_specs=(pl.BlockSpec((BLOCK, COLS), lambda i: (i, 0)), pl.BlockSpec((8, 128), lambda i: (0, 0))),
        out_shape=(shape((D, COLS), bf16), shape((8, 128), f32)),
        compiler_params=pltpu.CompilerParams(vmem_limit_bytes=20 * MB),
        cost_estimate=pl.CostEstimate(flops=2 * TOKENS * D * COLS, bytes_accessed=12 * MB, transcendentals=0),
    )(hidden, grad, after)


def add_four(a, b, c, d):
    return (a.astype(f32) + d.astype(f32)) + (b.astype(f32) + c.astype(f32))


def split_middle_kernel(a, b, c, d, after, *outs):
    for k, q in enumerate(outs):
        q[...] = add_four(a[k], b[k], c[k], d[k]).astype(q.dtype)


def split_middle(a, b, c, d, after):
    return call(
        split_middle_kernel,
        [shape((WIN, HALF), f32 if k == 0 else bf16) for k in range(4)],
        [VMEM] * 5,
        bytes_accessed=6 * MB,
    )(a, b, c, d, after)


def split_window_kernel(a, b, c, d, out, tok):
    total = add_four(a[...], b[...], c[...], d[...])
    for j in range(3):
        for r in range(16):
            tok[pl.ds(j * 16 + r, 16, stride=48), :] = total[j * 16:(j + 1) * 16, r * 128:(r + 1) * 128]
    for dev in range(16):
        out[dev] = tok[dev * 48:(dev + 1) * 48, :].astype(out.dtype)


def split_window(a, b, c, d):
    return call(
        split_window_kernel,
        shape((16, 48, 128), bf16),
        [VMEM] * 4,
        [pltpu.VMEM((768, 128), f32)],
    )(a, b, c, d)


def finish_kernel(parts, out, tok):
    for half in range(2):
        total = parts[half].astype(f32)
        for i in range(1, NZ):
            total += parts[2 * i + half].astype(f32)
        tok[...] = total
        for r in range(16):
            at = half * HALF + r * 128
            out[:, at:at + 128] = tok[pl.ds(r, 3, stride=16), :]


def finish(parts):
    return call(finish_kernel, shape((3, D), f32), [VMEM], [pltpu.VMEM((48, 128), f32)])(parts)


def local(hidden, head_weight, targets, image_mask, lengths, ref_logps, pairing):
    y, x, z, c = (lax.axis_index(a) for a in AXES)
    ids = jnp.stack([y, x, z, c, flat(y, x, z, c)]).astype(jnp.int32)

    digits = jnp.stack([targets % 256, targets // 256 % 256, targets // 65536], axis=1)
    meta = jnp.pad(digits.astype(f32).astype(bf16), ((0, 13), (0, 125)))
    halves = hidden.reshape(3, 2, 16, 128)
    first, second = (jnp.concatenate([halves[:, i].reshape(48, 128), meta], axis=0) for i in range(2))
    parts = lax.all_to_all(
        jnp.broadcast_to(jnp.stack([first, second])[None], (NZ, 2, 64, 128)).reshape(16, 64, 128),
        ("z", "c"), 0, 0, tiled=True,
    )
    block = join_window(ids, parts)
    blocks = join_blocks(block, *(fetch(block, middle(o)) for o in OFF[1:]))
    other = [fetch(blocks, near(1))]
    head, mark = load_head(head_weight)
    blocks = gate(blocks, other[0], mark)
    own = [blocks] + [fetch(blocks, final(o)) for o in OFF[1:]]
    other = other + [fetch(v, near(1)) for v in own[1:]]

    rows, logits, stats, target = local_logits(ids, own, other, head)
    stats = merge(exchange(stats, ("z", "c")))
    stats = lax.all_to_all(stats, ("y", "x"), 0, 0, tiled=True)
    log_norm, weight, loss = preference(stats, lengths, ref_logps, pairing)

    logit_grad, send = grad_other_first(ids, logits, log_norm, weight, target, head)
    received = [fetch(send, near(1))]
    received.append(fetch(grad_other_second(ids, logit_grad, head), near(1)))
    *parts, mark = grad_own(ids, logit_grad, head, received, arrived(received[0]))
    grad_head, mark = grad_head_of(rows, logit_grad, mark)
    parts = split_middle(parts[0], *(fetch(parts[s], final(-OFF[s])) for s in (1, 2, 3)), mark)
    parts = split_window(parts[0], *(fetch(parts[s], middle(-OFF[s])) for s in (1, 2, 3)))
    grad_hidden = finish(lax.all_to_all(parts, ("z", "c"), 0, 0, tiled=True))
    return grad_hidden.astype(bf16), grad_head, loss[0, 0]


def solution(mesh):
    fine = Mesh(mesh.devices.reshape(NY, NX, NZ, NC), AXES)
    return jax.shard_map(
        local,
        mesh=fine,
        in_specs=(P(AXES, None), P(None, AXES), P(AXES), P(AXES), P(), P(), P()),
        out_specs=(P(AXES, None), P(None, AXES), P()),
        check_vma=False,
    )
```

```python
import functools

import jax
import jax.numpy as jnp
from jax import lax
from jax.experimental import pallas as pl
from jax.experimental.pallas import tpu as pltpu
from jax.sharding import Mesh, PartitionSpec as P

V = 163840
CODES = 32768
WIN = 48
NEG = -1e30
BETA = 1.0
LOSS_SCALE = 4096.0

D = 4096
HALF = D // 2
COLS = 640
TOKENS = 768
META = 128
WIDE = HALF + META
NY, NX, NZ, NC = 4, 4, 8, 2
AXES = ("y", "x", "z", "c")
OFF = (0, 1, 3, 2)
bf16 = jnp.bfloat16
f32 = jnp.float32
VMEM = pl.BlockSpec(memory_space=pltpu.VMEM)
SMEM = pl.BlockSpec(memory_space=pltpu.SMEM)
HBM = pl.BlockSpec(memory_space=pltpu.HBM)
MB = 1024 * 1024
PIECE = HALF // 2


def flat(y, x, z, c):
    return ((y % NY * NX + x % NX) * NZ + z % NZ) * NC + c


def fetch(value, source):
    pairs = [
        (flat(*source(y, x, z, c)), flat(y, x, z, c))
        for y in range(NY) for x in range(NX) for z in range(NZ) for c in range(NC)
    ]
    return lax.ppermute(value, AXES, pairs)


def middle(step):
    return lambda y, x, z, c: (y + step, x, z, c) if c == 0 else (y, x + step, z, c)


def final(step):
    return lambda y, x, z, c: (y, x + step, z, c) if c == 0 else (y + step, x, z, c)


def near(y, x, z, c):
    return y, x, z, 1 - c


def window(ids, core, s, k):
    y, x = ids[0], ids[1]
    across = core == 0
    last = (jnp.where(across, x, y) + OFF[s]) % 4
    mid = (jnp.where(across, y, x) + OFF[k]) % 4
    return jnp.where(across, mid * NX + last, last * NX + mid)


def call(kernel, outs, ins, scratch=(), vmem=10, **cost):
    return pl.pallas_call(
        kernel,
        out_shape=outs,
        in_specs=ins,
        out_specs=jax.tree.map(lambda _: VMEM, outs),
        scratch_shapes=list(scratch),
        compiler_params=pltpu.CompilerParams(vmem_limit_bytes=vmem * MB),
        cost_estimate=pl.CostEstimate(
            flops=cost.get("flops", 0), bytes_accessed=cost.get("bytes_accessed", 0), transcendentals=0
        ),
    )


def shape(dims, dtype):
    return jax.ShapeDtypeStruct(dims, dtype)


def join_window_kernel(ids, parts, out, tok, meta):
    for dev in range(16):
        tok[dev * 48:(dev + 1) * 48, :] = parts[dev, 0:48, :].astype(f32)
        meta[dev * 16:(dev + 1) * 16, :] = parts[dev, 48:64, :].astype(f32)
    for j in range(3):
        for r in range(16):
            out[j * 16:(j + 1) * 16, r * 128:(r + 1) * 128] = tok[pl.ds(j * 16 + r, 16, stride=48), :].astype(bf16)
        out[j * 16:(j + 1) * 16, HALF:WIDE] = meta[pl.ds(j, 16, stride=16), :].astype(bf16)


def join_window(ids, parts):
    return call(
        join_window_kernel,
        shape((WIN, WIDE), bf16),
        [SMEM, VMEM],
        [pltpu.VMEM((768, 128), f32), pltpu.VMEM((256, 128), f32)],
    )(ids, parts)


def join_blocks_kernel(a, b, c, d, low, high):
    low[0], low[1], high[0], high[1] = a[...], b[...], c[...], d[...]


def join_blocks(*blocks):
    return call(join_blocks_kernel, [shape((2, WIN, WIDE), bf16)] * 2, [VMEM] * 4)(*blocks)


def gate_kernel(low, high, first, second, third, out_low, out_high):
    out_low[...] = low[...]
    out_high[...] = high[...]


def gate(low, high, *marks):
    return call(gate_kernel, [shape(low.shape, low.dtype)] * 2, [VMEM] * 5)(low, high, *marks)


def columns_of(rows):
    full = jnp.concatenate([rows, jnp.zeros((128 - rows.shape[0], 128), f32)], axis=0)
    return full.T


def load_kernel(head_hbm, head, mark, sem):
    mark[...] = jnp.zeros_like(mark)
    copy = pltpu.make_async_copy(head_hbm, head, sem)
    copy.start()
    copy.wait()


def load_head(head):
    return call(
        load_kernel,
        (shape((D, COLS), bf16), shape((8, 128), f32)),
        [HBM],
        [pltpu.SemaphoreType.DMA],
        vmem=8,
        bytes_accessed=10 * MB,
    )(head)


def logits_kernel(
    ids, *refs
):
    own_blocks, other_blocks = refs[:8], refs[8:16]
    head, hidden, logits, stats, target, meta, cols = refs[16:]
    rows = 256
    core = ids[3]
    own = pl.multiple_of(core * HALF, HALF)
    oth = pl.multiple_of((1 - core) * HALF, HALF)
    for i, (a, b) in enumerate(zip(own_blocks, other_blocks)):
        for inner in range(2):
            s, k = i // 2, i % 2 * 2 + inner
            row = pl.multiple_of(window(ids, core, s, k) * WIN, 16)
            hidden[pl.ds(row, WIN), pl.ds(own, HALF)] = a[inner, :, 0:HALF]
            meta[pl.ds(row, WIN), :] = a[inner, :, HALF:WIDE].astype(f32)
            row = pl.multiple_of(window(ids, 1 - core, s, k) * WIN, 16)
            hidden[pl.ds(row, WIN), pl.ds(oth, HALF)] = b[inner, :, 0:HALF]
    first = ids[4] * COLS
    column = first + lax.broadcasted_iota(jnp.int32, (rows, COLS), 1)
    lane = lax.broadcasted_iota(jnp.int32, (rows, 128), 1)
    for i in range(TOKENS // rows):
        at = pl.ds(i * rows, rows)
        part = jnp.dot(hidden[at, :], head[...], preferred_element_type=f32)
        logits[at, :] = part
        digits = meta[at, :]
        goal = (digits[:, 0:1] + 256.0 * digits[:, 1:2] + 65536.0 * digits[:, 2:3]).astype(jnp.int32)
        in_range = (goal >= V - CODES) == (column >= V - CODES)
        masked = jnp.where(in_range, part, NEG)
        peak = jnp.max(masked, axis=1, keepdims=True)
        total = jnp.sum(jnp.where(in_range, jnp.exp(masked - peak), 0.0), axis=1, keepdims=True)
        hit = jnp.sum(jnp.where(column == goal, part, 0.0), axis=1, keepdims=True)
        norm = peak + jnp.log(jnp.maximum(total, 1e-37))
        cols[at, :] = jnp.where(lane == 0, norm, jnp.where(lane == 1, hit, goal.astype(f32)))
    stats[...] = jnp.zeros_like(stats)
    target[...] = jnp.zeros_like(target)
    for b in range(TOKENS // 128):
        turned = cols[b * 128:(b + 1) * 128, :].T
        for i in range(2):
            stats[i, b:b + 1, :] = turned[i:i + 1, :]
        target[b:b + 1, :] = turned[2:3, :]


def local_logits(ids, own, other, head):
    return pl.pallas_call(
        logits_kernel,
        out_shape=(
            shape((TOKENS, D), bf16),
            shape((TOKENS, COLS), f32),
            shape((2, 8, 128), f32),
            shape((8, 128), f32),
        ),
        in_specs=[SMEM] + [VMEM] * 17,
        out_specs=(VMEM, VMEM, VMEM, VMEM),
        scratch_shapes=[
            pltpu.VMEM((TOKENS, 128), f32),
            pltpu.VMEM((TOKENS, 128), f32),
        ],
        compiler_params=pltpu.CompilerParams(vmem_limit_bytes=25 * MB),
        cost_estimate=pl.CostEstimate(flops=2 * TOKENS * D * COLS, bytes_accessed=20 * MB, transcendentals=0),
    )(ids, *own, *other, head)


def exchange(value, axes):
    return lax.all_to_all(jnp.broadcast_to(value[None], (16,) + value.shape), axes, 0, 0, tiled=True)


def merged(parts):
    peak = parts[0, 0]
    for i in range(1, 16):
        peak = jnp.maximum(peak, parts[i, 0])
    total = jnp.zeros_like(peak)
    hit = jnp.zeros_like(peak)
    for i in range(16):
        total += jnp.exp(parts[i, 0] - peak)
        hit += parts[i, 1]
    return peak + jnp.log(total), hit


def merge_kernel(parts, out):
    norm, hit = merged(parts)
    for i in range(16):
        out[i, 0], out[i, 1] = norm, hit


def merge(parts):
    return call(merge_kernel, shape((16, 2, 8, 128), f32), [VMEM])(parts)


def preference_kernel(parts, lengths, ref_logps, pairing, norm, weight, loss):
    log_norm, hit = merged(parts)
    token_lp = hit - log_norm
    rows = lax.broadcasted_iota(jnp.int32, (8, 128), 0) * 128 + lax.broadcasted_iota(jnp.int32, (8, 128), 1)
    inner = rows % WIN
    group, position = rows // WIN, inner % 16 * 3 + inner // 16
    pairs = pairing.shape[0] // 2
    token_weight = jnp.zeros((8, 128), f32)
    losses = jnp.zeros((1, 1), f32)
    for k in range(pairs):
        sides = []
        for g in (pairing[2 * k], pairing[2 * k + 1]):
            count = lengths[g].astype(f32)
            live = (group == g) & (position < lengths[g])
            policy = jnp.sum(jnp.where(live, token_lp, 0.0), keepdims=True) / count
            sides.append((live, count, policy - ref_logps[g]))
        (live_c, count_c, chosen), (live_r, count_r, rejected) = sides
        margin = BETA * (chosen - rejected)
        losses += jnp.maximum(-margin, 0.0) + jnp.log1p(jnp.exp(-jnp.abs(margin)))
        pair_weight = -LOSS_SCALE * BETA * jax.nn.sigmoid(-margin) / pairs
        token_weight += jnp.where(live_c, pair_weight / count_c, 0.0)
        token_weight -= jnp.where(live_r, pair_weight / count_r, 0.0)
    norm[...] = log_norm
    weight[...] = token_weight
    loss[...] = jnp.broadcast_to(losses / pairs, (8, 128))


def preference(parts, lengths, ref_logps, pairing):
    return call(
        preference_kernel,
        [shape((8, 128), f32)] * 3,
        [VMEM, SMEM, SMEM, SMEM],
    )(parts, lengths, ref_logps, pairing)


BLOCK = 512
STEP = 256


def times_head(grad, rows):
    return lax.dot_general(grad, rows, (((1,), (1,)), ((), ())), preferred_element_type=f32)


def head_rows(half, start):
    return pl.ds(pl.multiple_of(half * HALF + start, STEP), STEP)


def other_piece(piece, ids, grad, head, out):
    for i in range(PIECE // STEP):
        rows = head[head_rows(1 - ids[3], piece * PIECE + i * STEP), :]
        out[:, i * STEP:(i + 1) * STEP] = times_head(grad[...], rows).astype(out.dtype)


def grad_other_first_kernel(ids, logits, norm, weight, target, head, grad, out):
    norm_c, weight_c, goal_c = columns_of(norm[...]), columns_of(weight[...]), columns_of(target[...])
    column = ids[4] * COLS + lax.broadcasted_iota(jnp.int32, (128, COLS), 1)
    for b in range(TOKENS // 128):
        goal = goal_c[:, b:b + 1].astype(jnp.int32)
        in_range = (goal >= V - CODES) == (column >= V - CODES)
        at = slice(b * 128, (b + 1) * 128)
        prob = jnp.exp(jnp.where(in_range, logits[at, :] - norm_c[:, b:b + 1], NEG))
        grad[at, :] = (weight_c[:, b:b + 1] * ((column == goal).astype(f32) - prob)).astype(bf16)
    other_piece(0, ids, grad, head, out)


def grad_other_first(ids, logits, norm, weight, target, head):
    return call(
        grad_other_first_kernel,
        (shape((TOKENS, COLS), bf16), shape((TOKENS, PIECE), bf16)),
        [SMEM] + [VMEM] * 5,
        vmem=16,
        flops=TOKENS * PIECE * COLS * 2,
        bytes_accessed=6 * MB,
    )(ids, logits, norm, weight, target, head)


def grad_other_second(ids, grad, head):
    return call(
        functools.partial(other_piece, 1),
        shape((TOKENS, PIECE), bf16),
        [SMEM, VMEM, VMEM],
        vmem=16,
        flops=TOKENS * PIECE * COLS * 4,
        bytes_accessed=16 * MB,
    )(ids, grad, head)


def arrived_kernel(value, mark):
    mark[...] = jnp.zeros_like(mark)


def arrived(value):
    return call(arrived_kernel, shape((8, 128), f32), [VMEM], vmem=4)(value)


def grad_own_kernel(ids, grad, head, other0, other1, after, *refs):
    parts, mark, total = refs[:8], refs[8], refs[9]
    mark[...] = jnp.zeros_like(mark)
    for i in range(HALF // STEP):
        at = slice(i * STEP, (i + 1) * STEP)
        other = (other0, other1)[i * STEP // PIECE]
        inner = i * STEP % PIECE
        total[...] = times_head(grad[...], head[head_rows(ids[3], i * STEP), :])
        total[...] += other[:, inner:inner + STEP].astype(f32)
        for n, r in enumerate(parts):
            for inner in range(2):
                row = pl.multiple_of(window(ids, ids[3], n // 2, n % 2 * 2 + inner) * WIN, 16)
                r[inner, :, at] = total[pl.ds(row, WIN), :].astype(r.dtype)


PART_TYPES = (f32, f32, f32, bf16, bf16, f32, bf16, bf16)


def grad_own(ids, grad, head, other, after):
    return call(
        grad_own_kernel,
        [shape((2, WIN, HALF), t) for t in PART_TYPES] + [shape((8, 128), f32)],
        [SMEM] + [VMEM] * 5,
        [pltpu.VMEM((TOKENS, STEP), f32)],
        vmem=22,
    )(ids, grad, head, *other, after)


def head_kernel(hidden, grad, after, out, mark):
    mark[...] = jnp.zeros_like(mark)
    out[...] = lax.dot_general(
        hidden[...], grad[...], (((0,), (0,)), ((), ())), preferred_element_type=f32
    ).astype(out.dtype)


def grad_head_of(hidden, grad, after):
    return pl.pallas_call(
        head_kernel,
        grid=(D // BLOCK,),
        in_specs=[
            pl.BlockSpec((TOKENS, BLOCK), lambda i: (0, i)),
            pl.BlockSpec((TOKENS, COLS), lambda i: (0, 0)),
            pl.BlockSpec((8, 128), lambda i: (0, 0)),
        ],
        out_specs=(pl.BlockSpec((BLOCK, COLS), lambda i: (i, 0)), pl.BlockSpec((8, 128), lambda i: (0, 0))),
        out_shape=(shape((D, COLS), bf16), shape((8, 128), f32)),
        compiler_params=pltpu.CompilerParams(vmem_limit_bytes=20 * MB),
        cost_estimate=pl.CostEstimate(flops=2 * TOKENS * D * COLS, bytes_accessed=12 * MB, transcendentals=0),
    )(hidden, grad, after)


def add_four(a, b, c, d):
    return (a.astype(f32) + d.astype(f32)) + (b.astype(f32) + c.astype(f32))


def add_kernel(a, b, out):
    out[...] = (a[...] + b[...].astype(f32)).astype(out.dtype)


def add(a, b):
    return call(add_kernel, shape(a.shape, bf16), [VMEM] * 2)(a, b)


def split_middle_kernel(*refs):
    ins, outs = refs[:6], refs[7:]
    for k, q in enumerate(outs):
        own, back, ahead = (ins[3 * (k // 2) + i][k % 2].astype(f32) for i in range(3))
        q[...] = (own + (back + ahead)).astype(q.dtype)


def split_middle(low, high, after):
    return call(
        split_middle_kernel,
        [shape((WIN, HALF), f32 if k == 0 else bf16) for k in range(4)],
        [VMEM] * 7,
        bytes_accessed=6 * MB,
    )(*low, *high, after)


def split_window_kernel(a, b, c, d, out, tok):
    total = add_four(a[...], b[...], c[...], d[...])
    for j in range(3):
        for r in range(16):
            tok[pl.ds(j * 16 + r, 16, stride=48), :] = total[j * 16:(j + 1) * 16, r * 128:(r + 1) * 128]
    for dev in range(16):
        out[dev] = tok[dev * 48:(dev + 1) * 48, :].astype(out.dtype)


def split_window(a, b, c, d):
    return call(
        split_window_kernel,
        shape((16, 48, 128), bf16),
        [VMEM] * 4,
        [pltpu.VMEM((768, 128), f32)],
    )(a, b, c, d)


def finish_kernel(parts, out, tok):
    for half in range(2):
        total = parts[half].astype(f32)
        for i in range(1, NZ):
            total += parts[2 * i + half].astype(f32)
        tok[...] = total
        for r in range(16):
            at = half * HALF + r * 128
            out[:, at:at + 128] = tok[pl.ds(r, 3, stride=16), :]


def finish(parts):
    return call(finish_kernel, shape((3, D), f32), [VMEM], [pltpu.VMEM((48, 128), f32)])(parts)


def local(hidden, head_weight, targets, image_mask, lengths, ref_logps, pairing):
    y, x, z, c = (lax.axis_index(a) for a in AXES)
    ids = jnp.stack([y, x, z, c, flat(y, x, z, c)]).astype(jnp.int32)

    digits = jnp.stack([targets % 256, targets // 256 % 256, targets // 65536], axis=1)
    meta = jnp.pad(digits.astype(f32).astype(bf16), ((0, 13), (0, 125)))
    halves = hidden.reshape(3, 2, 16, 128)
    first, second = (jnp.concatenate([halves[:, i].reshape(48, 128), meta], axis=0) for i in range(2))
    parts = lax.all_to_all(
        jnp.broadcast_to(jnp.stack([first, second])[None], (NZ, 2, 64, 128)).reshape(16, 64, 128),
        ("z", "c"), 0, 0, tiled=True,
    )
    block = join_window(ids, parts)
    low, high = join_blocks(block, *(fetch(block, middle(o)) for o in OFF[1:]))
    other = [fetch(low, near), fetch(high, near)]
    head, mark = load_head(head_weight)
    low, high = gate(low, high, *other, mark)
    ahead_low, back_high = fetch(low, final(1)), fetch(high, final(-1))
    ahead_high, back_low = fetch(high, final(1)), fetch(low, final(-1))
    far_low, far_high = fetch(ahead_low, final(1)), fetch(back_high, final(-1))
    own = [low, high, ahead_low, ahead_high, back_low, back_high, far_low, far_high]
    other += [fetch(v, near) for v in own[2:]]

    rows, logits, stats, target = local_logits(ids, own, other, head)
    stats = merge(exchange(stats, ("z", "c")))
    stats = lax.all_to_all(stats, ("y", "x"), 0, 0, tiled=True)
    log_norm, weight, loss = preference(stats, lengths, ref_logps, pairing)

    logit_grad, send = grad_other_first(ids, logits, log_norm, weight, target, head)
    received = [fetch(send, near)]
    received.append(fetch(grad_other_second(ids, logit_grad, head), near))
    *parts, mark = grad_own(ids, logit_grad, head, received, arrived(received[0]))
    grad_head, mark = grad_head_of(rows, logit_grad, mark)
    keep_low, keep_high, ahead_low, ahead_high, back_low, back_high, far_low, far_high = parts
    ahead_low = add(ahead_low, fetch(far_low, final(-1)))
    back_high = add(back_high, fetch(far_high, final(1)))
    parts = split_middle(
        (keep_low, fetch(ahead_low, final(-1)), fetch(back_low, final(1))),
        (keep_high, fetch(ahead_high, final(-1)), fetch(back_high, final(1))),
        mark,
    )
    parts = split_window(parts[0], *(fetch(parts[s], middle(-OFF[s])) for s in (1, 2, 3)))
    grad_hidden = finish(lax.all_to_all(parts, ("z", "c"), 0, 0, tiled=True))
    return grad_hidden.astype(bf16), grad_head, loss[0, 0]


def solution(mesh):
    fine = Mesh(mesh.devices.reshape(NY, NX, NZ, NC), AXES)
    return jax.shard_map(
        local,
        mesh=fine,
        in_specs=(P(AXES, None), P(None, AXES), P(AXES), P(AXES), P(), P(), P()),
        out_specs=(P(AXES, None), P(None, AXES), P()),
        check_vma=False,
    )
```

```python
import functools

import jax
import jax.numpy as jnp
from jax import lax
from jax.experimental import pallas as pl
from jax.experimental.pallas import tpu as pltpu
from jax.sharding import Mesh, PartitionSpec as P

V = 163840
CODES = 32768
WIN = 48
NEG = -1e30
BETA = 1.0
LOSS_SCALE = 4096.0

D = 4096
HALF = D // 2
COLS = 640
TOKENS = 768
META = 128
WIDE = HALF + META
NY, NX, NZ, NC = 4, 4, 8, 2
AXES = ("y", "x", "z", "c")
OFF = (0, 1, 3, 2)
bf16 = jnp.bfloat16
f32 = jnp.float32
VMEM = pl.BlockSpec(memory_space=pltpu.VMEM)
SMEM = pl.BlockSpec(memory_space=pltpu.SMEM)
HBM = pl.BlockSpec(memory_space=pltpu.HBM)
MB = 1024 * 1024
PIECE = HALF // 2


def flat(y, x, z, c):
    return ((y % NY * NX + x % NX) * NZ + z % NZ) * NC + c


def fetch(value, source):
    pairs = [
        (flat(*source(y, x, z, c)), flat(y, x, z, c))
        for y in range(NY) for x in range(NX) for z in range(NZ) for c in range(NC)
    ]
    return lax.ppermute(value, AXES, pairs)


def middle(step):
    return lambda y, x, z, c: (y + step, x, z, c) if c == 0 else (y, x + step, z, c)


def final(step):
    return lambda y, x, z, c: (y, x + step, z, c) if c == 0 else (y + step, x, z, c)


def near(y, x, z, c):
    return y, x, z, 1 - c


def window(ids, core, s, k):
    y, x = ids[0], ids[1]
    across = core == 0
    last = (jnp.where(across, x, y) + OFF[s]) % 4
    mid = (jnp.where(across, y, x) + OFF[k]) % 4
    return jnp.where(across, mid * NX + last, last * NX + mid)


def call(kernel, outs, ins, scratch=(), vmem=10, **cost):
    return pl.pallas_call(
        kernel,
        out_shape=outs,
        in_specs=ins,
        out_specs=jax.tree.map(lambda _: VMEM, outs),
        scratch_shapes=list(scratch),
        compiler_params=pltpu.CompilerParams(vmem_limit_bytes=vmem * MB),
        cost_estimate=pl.CostEstimate(
            flops=cost.get("flops", 0), bytes_accessed=cost.get("bytes_accessed", 0), transcendentals=0
        ),
    )


def shape(dims, dtype):
    return jax.ShapeDtypeStruct(dims, dtype)


def first_message_kernel(targets, hidden, out, tok):
    rows = hidden[...].astype(f32)
    row = lax.broadcasted_iota(jnp.int32, (16, 128), 0)
    lane = lax.broadcasted_iota(jnp.int32, (16, 128), 1)
    meta = jnp.zeros((16, 128), f32)
    for j in range(3):
        goal = targets[j]
        for n, digit in enumerate((goal & 255, (goal >> 8) & 255, goal >> 16)):
            meta = jnp.where((row == j) & (lane == n), digit.astype(f32), meta)
    meta = meta.astype(bf16)
    for half in range(2):
        for r in range(16):
            at = half * HALF + r * 128
            tok[pl.ds(r, 3, stride=16), :] = rows[:, at:at + 128]
        part = tok[...].astype(bf16)
        for z in range(NZ):
            out[2 * z + half, 0:48, :] = part
            out[2 * z + half, 48:64, :] = meta


def first_message(targets, hidden):
    return call(
        first_message_kernel, shape((16, 64, 128), bf16), [SMEM, VMEM], [pltpu.VMEM((48, 128), f32)]
    )(targets, hidden)


def join_window_kernel(ids, parts, out, tok, meta):
    for dev in range(16):
        tok[dev * 48:(dev + 1) * 48, :] = parts[dev, 0:48, :].astype(f32)
        meta[dev * 16:(dev + 1) * 16, :] = parts[dev, 48:64, :].astype(f32)
    for j in range(3):
        for r in range(16):
            out[j * 16:(j + 1) * 16, r * 128:(r + 1) * 128] = tok[pl.ds(j * 16 + r, 16, stride=48), :].astype(bf16)
        out[j * 16:(j + 1) * 16, HALF:WIDE] = meta[pl.ds(j, 16, stride=16), :].astype(bf16)


def join_window(ids, parts):
    return call(
        join_window_kernel,
        shape((WIN, WIDE), bf16),
        [SMEM, VMEM],
        [pltpu.VMEM((768, 128), f32), pltpu.VMEM((256, 128), f32)],
    )(ids, parts)


def join_blocks_kernel(a, b, c, d, after, low, high):
    low[0], low[1], high[0], high[1] = a[...], b[...], c[...], d[...]


def join_blocks(*blocks):
    return call(join_blocks_kernel, [shape((2, WIN, WIDE), bf16)] * 2, [VMEM] * 5)(*blocks)


def gate_kernel(low, high, first, second, out_low, out_high):
    out_low[...] = low[...]
    out_high[...] = high[...]


def gate(low, high, *marks):
    return call(gate_kernel, [shape(low.shape, low.dtype)] * 2, [VMEM] * 4)(low, high, *marks)


def columns_of(rows):
    full = jnp.concatenate([rows, jnp.zeros((128 - rows.shape[0], 128), f32)], axis=0)
    return full.T


def load_kernel(head_hbm, head, mark, sem):
    mark[...] = jnp.zeros_like(mark)
    copy = pltpu.make_async_copy(head_hbm, head, sem)
    copy.start()
    copy.wait()


def load_head(head):
    return call(
        load_kernel,
        (shape((D, COLS), bf16), shape((8, 128), f32)),
        [HBM],
        [pltpu.SemaphoreType.DMA],
        vmem=8,
        bytes_accessed=10 * MB,
    )(head)


def logits_kernel(
    ids, *refs
):
    own_blocks, other_blocks = refs[:8], refs[8:16]
    head, hidden, logits, stats, target, meta, cols = refs[16:]
    rows = 256
    core = ids[3]
    own = pl.multiple_of(core * HALF, HALF)
    oth = pl.multiple_of((1 - core) * HALF, HALF)
    for i, (a, b) in enumerate(zip(own_blocks, other_blocks)):
        for inner in range(2):
            s, k = i // 2, i % 2 * 2 + inner
            row = pl.multiple_of(window(ids, core, s, k) * WIN, 16)
            hidden[pl.ds(row, WIN), pl.ds(own, HALF)] = a[inner, :, 0:HALF]
            meta[pl.ds(row, WIN), :] = a[inner, :, HALF:WIDE].astype(f32)
            row = pl.multiple_of(window(ids, 1 - core, s, k) * WIN, 16)
            hidden[pl.ds(row, WIN), pl.ds(oth, HALF)] = b[inner, :, 0:HALF]
    first = ids[4] * COLS
    column = first + lax.broadcasted_iota(jnp.int32, (rows, COLS), 1)
    lane = lax.broadcasted_iota(jnp.int32, (rows, 128), 1)
    for i in range(TOKENS // rows):
        at = pl.ds(i * rows, rows)
        part = jnp.dot(hidden[at, :], head[...], preferred_element_type=f32)
        logits[at, :] = part
        digits = meta[at, :]
        goal = (digits[:, 0:1] + 256.0 * digits[:, 1:2] + 65536.0 * digits[:, 2:3]).astype(jnp.int32)
        in_range = (goal >= V - CODES) == (column >= V - CODES)
        masked = jnp.where(in_range, part, NEG)
        peak = jnp.max(masked, axis=1, keepdims=True)
        total = jnp.sum(jnp.where(in_range, jnp.exp(masked - peak), 0.0), axis=1, keepdims=True)
        hit = jnp.sum(jnp.where(column == goal, part, 0.0), axis=1, keepdims=True)
        norm = peak + jnp.log(jnp.maximum(total, 1e-37))
        cols[at, :] = jnp.where(lane == 0, norm, jnp.where(lane == 1, hit, goal.astype(f32)))
    stats[...] = jnp.zeros_like(stats)
    target[...] = jnp.zeros_like(target)
    for b in range(TOKENS // 128):
        turned = cols[b * 128:(b + 1) * 128, :].T
        for i in range(2):
            stats[i, b:b + 1, :] = turned[i:i + 1, :]
        target[b:b + 1, :] = turned[2:3, :]


def local_logits(ids, own, other, head):
    return pl.pallas_call(
        logits_kernel,
        out_shape=(
            shape((TOKENS, D), bf16),
            shape((TOKENS, COLS), f32),
            shape((2, 8, 128), f32),
            shape((8, 128), f32),
        ),
        in_specs=[SMEM] + [VMEM] * 17,
        out_specs=(VMEM, VMEM, VMEM, VMEM),
        scratch_shapes=[
            pltpu.VMEM((TOKENS, 128), f32),
            pltpu.VMEM((TOKENS, 128), f32),
        ],
        compiler_params=pltpu.CompilerParams(vmem_limit_bytes=25 * MB),
        cost_estimate=pl.CostEstimate(flops=2 * TOKENS * D * COLS, bytes_accessed=20 * MB, transcendentals=0),
    )(ids, *own, *other, head)


def exchange(value, axes):
    return lax.all_to_all(jnp.broadcast_to(value[None], (16,) + value.shape), axes, 0, 0, tiled=True)


def merged(parts):
    peak = parts[0, 0]
    for i in range(1, 16):
        peak = jnp.maximum(peak, parts[i, 0])
    total = jnp.zeros_like(peak)
    hit = jnp.zeros_like(peak)
    for i in range(16):
        total += jnp.exp(parts[i, 0] - peak)
        hit += parts[i, 1]
    return peak + jnp.log(total), hit


def merge_kernel(parts, out):
    norm, hit = merged(parts)
    for i in range(16):
        out[i, 0], out[i, 1] = norm, hit


def merge(parts):
    return call(merge_kernel, shape((16, 2, 8, 128), f32), [VMEM])(parts)


def preference_kernel(parts, lengths, ref_logps, pairing, norm, weight, loss):
    log_norm, hit = merged(parts)
    token_lp = hit - log_norm
    rows = lax.broadcasted_iota(jnp.int32, (8, 128), 0) * 128 + lax.broadcasted_iota(jnp.int32, (8, 128), 1)
    inner = rows % WIN
    group, position = rows // WIN, inner % 16 * 3 + inner // 16
    pairs = pairing.shape[0] // 2
    token_weight = jnp.zeros((8, 128), f32)
    losses = jnp.zeros((1, 1), f32)
    for k in range(pairs):
        sides = []
        for g in (pairing[2 * k], pairing[2 * k + 1]):
            count = lengths[g].astype(f32)
            live = (group == g) & (position < lengths[g])
            policy = jnp.sum(jnp.where(live, token_lp, 0.0), keepdims=True) / count
            sides.append((live, count, policy - ref_logps[g]))
        (live_c, count_c, chosen), (live_r, count_r, rejected) = sides
        margin = BETA * (chosen - rejected)
        losses += jnp.maximum(-margin, 0.0) + jnp.log1p(jnp.exp(-jnp.abs(margin)))
        pair_weight = -LOSS_SCALE * BETA * jax.nn.sigmoid(-margin) / pairs
        token_weight += jnp.where(live_c, pair_weight / count_c, 0.0)
        token_weight -= jnp.where(live_r, pair_weight / count_r, 0.0)
    norm[...] = log_norm
    weight[...] = token_weight
    loss[...] = jnp.broadcast_to(losses / pairs, (8, 128))


def preference(parts, lengths, ref_logps, pairing):
    return call(
        preference_kernel,
        [shape((8, 128), f32)] * 3,
        [VMEM, SMEM, SMEM, SMEM],
    )(parts, lengths, ref_logps, pairing)


BLOCK = 512
STEP = 256


def times_head(grad, rows):
    return lax.dot_general(grad, rows, (((1,), (1,)), ((), ())), preferred_element_type=f32)


def head_rows(half, start):
    return pl.ds(pl.multiple_of(half * HALF + start, STEP), STEP)


def other_piece(piece, ids, grad, head, out):
    for i in range(PIECE // STEP):
        rows = head[head_rows(1 - ids[3], piece * PIECE + i * STEP), :]
        out[:, i * STEP:(i + 1) * STEP] = times_head(grad[...], rows).astype(out.dtype)


def grad_other_first_kernel(ids, logits, norm, weight, target, head, grad, out):
    norm_c, weight_c, goal_c = columns_of(norm[...]), columns_of(weight[...]), columns_of(target[...])
    column = ids[4] * COLS + lax.broadcasted_iota(jnp.int32, (128, COLS), 1)
    for b in range(TOKENS // 128):
        goal = goal_c[:, b:b + 1].astype(jnp.int32)
        in_range = (goal >= V - CODES) == (column >= V - CODES)
        at = slice(b * 128, (b + 1) * 128)
        prob = jnp.exp(jnp.where(in_range, logits[at, :] - norm_c[:, b:b + 1], NEG))
        grad[at, :] = (weight_c[:, b:b + 1] * ((column == goal).astype(f32) - prob)).astype(bf16)
    other_piece(0, ids, grad, head, out)


def grad_other_first(ids, logits, norm, weight, target, head):
    return call(
        grad_other_first_kernel,
        (shape((TOKENS, COLS), bf16), shape((TOKENS, PIECE), bf16)),
        [SMEM] + [VMEM] * 5,
        vmem=16,
        flops=TOKENS * PIECE * COLS * 2,
        bytes_accessed=6 * MB,
    )(ids, logits, norm, weight, target, head)


def grad_other_second(ids, grad, head):
    return call(
        functools.partial(other_piece, 1),
        shape((TOKENS, PIECE), bf16),
        [SMEM, VMEM, VMEM],
        vmem=16,
        flops=TOKENS * PIECE * COLS * 4,
        bytes_accessed=16 * MB,
    )(ids, grad, head)


def arrived_kernel(value, mark):
    mark[...] = jnp.zeros_like(mark)


def arrived(value):
    return call(arrived_kernel, shape((8, 128), f32), [VMEM], vmem=4)(value)


def grad_own_kernel(ids, grad, head, other0, other1, after, *refs):
    parts, mark, total = refs[:8], refs[8], refs[9]
    mark[...] = jnp.zeros_like(mark)
    for i in range(HALF // STEP):
        at = slice(i * STEP, (i + 1) * STEP)
        other = (other0, other1)[i * STEP // PIECE]
        inner = i * STEP % PIECE
        total[...] = times_head(grad[...], head[head_rows(ids[3], i * STEP), :])
        total[...] += other[:, inner:inner + STEP].astype(f32)
        for n, r in enumerate(parts):
            for inner in range(2):
                row = pl.multiple_of(window(ids, ids[3], n // 2, n % 2 * 2 + inner) * WIN, 16)
                r[inner, :, at] = total[pl.ds(row, WIN), :].astype(r.dtype)


PART_TYPES = (f32, f32, f32, bf16, bf16, f32, bf16, bf16)


def grad_own(ids, grad, head, other, after):
    return call(
        grad_own_kernel,
        [shape((2, WIN, HALF), t) for t in PART_TYPES] + [shape((8, 128), f32)],
        [SMEM] + [VMEM] * 5,
        [pltpu.VMEM((TOKENS, STEP), f32)],
        vmem=22,
    )(ids, grad, head, *other, after)


def head_kernel(hidden, grad, *refs):
    out, mark = refs[-2:]
    mark[...] = jnp.zeros_like(mark)
    out[...] = lax.dot_general(
        hidden[...], grad[...], (((0,), (0,)), ((), ())), preferred_element_type=f32
    ).astype(out.dtype)


def grad_head_half(hidden, grad, after, first=None):
    steps = D // BLOCK // 2
    base = 0 if first is None else steps
    return pl.pallas_call(
        head_kernel,
        grid=(steps,),
        in_specs=[
            pl.BlockSpec((TOKENS, BLOCK), lambda i: (0, i + base)),
            pl.BlockSpec((TOKENS, COLS), lambda i: (0, 0)),
            pl.BlockSpec((8, 128), lambda i: (0, 0)),
        ] + ([] if first is None else [pl.BlockSpec(memory_space=pl.ANY)]),
        out_specs=(pl.BlockSpec((BLOCK, COLS), lambda i: (i + base, 0)), pl.BlockSpec((8, 128), lambda i: (0, 0))),
        out_shape=(shape((D, COLS), bf16), shape((8, 128), f32)),
        input_output_aliases={} if first is None else {3: 0},
        compiler_params=pltpu.CompilerParams(vmem_limit_bytes=20 * MB),
        cost_estimate=pl.CostEstimate(flops=TOKENS * D * COLS, bytes_accessed=6 * MB, transcendentals=0),
    )(hidden, grad, after, *([] if first is None else [first]))


def add_four(a, b, c, d):
    return (a.astype(f32) + d.astype(f32)) + (b.astype(f32) + c.astype(f32))


def add_kernel(a, b, after, out, mark):
    mark[...] = jnp.zeros_like(mark)
    out[...] = (a[...] + b[...].astype(f32)).astype(out.dtype)


def add(a, b, after):
    return call(add_kernel, (shape(a.shape, bf16), shape((8, 128), f32)), [VMEM] * 3)(a, b, after)


def split_middle_kernel(*refs):
    ins, outs = refs[:6], refs[7:]
    for k, q in enumerate(outs):
        own, back, ahead = (ins[3 * (k // 2) + i][k % 2].astype(f32) for i in range(3))
        q[...] = (own + (back + ahead)).astype(q.dtype)


def split_middle(low, high, after):
    return call(
        split_middle_kernel,
        [shape((WIN, HALF), f32 if k == 0 else bf16) for k in range(4)],
        [VMEM] * 7,
        bytes_accessed=6 * MB,
    )(*low, *high, after)


def split_window_kernel(a, b, c, d, out, tok):
    total = add_four(a[...], b[...], c[...], d[...])
    for j in range(3):
        for r in range(16):
            tok[pl.ds(j * 16 + r, 16, stride=48), :] = total[j * 16:(j + 1) * 16, r * 128:(r + 1) * 128]
    for dev in range(16):
        out[dev] = tok[dev * 48:(dev + 1) * 48, :].astype(out.dtype)


def split_window(a, b, c, d):
    return call(
        split_window_kernel,
        shape((16, 48, 128), bf16),
        [VMEM] * 4,
        [pltpu.VMEM((768, 128), f32)],
    )(a, b, c, d)


def finish_kernel(parts, out, tok):
    for half in range(2):
        total = parts[half].astype(f32)
        for i in range(1, NZ):
            total += parts[2 * i + half].astype(f32)
        tok[...] = total
        for r in range(16):
            at = half * HALF + r * 128
            out[:, at:at + 128] = tok[pl.ds(r, 3, stride=16), :].astype(bf16)


def finish(parts):
    return call(finish_kernel, shape((3, D), bf16), [VMEM], [pltpu.VMEM((48, 128), f32)])(parts)


def local(hidden, head_weight, targets, image_mask, lengths, ref_logps, pairing):
    y, x, z, c = (lax.axis_index(a) for a in AXES)
    ids = jnp.stack([y, x, z, c, flat(y, x, z, c)]).astype(jnp.int32)

    parts = lax.all_to_all(first_message(targets, hidden), ("z", "c"), 0, 0, tiled=True)
    block = join_window(ids, parts)
    head, mark = load_head(head_weight)
    low, high = join_blocks(block, *(fetch(block, middle(o)) for o in OFF[1:]), mark)
    other = [fetch(low, near), fetch(high, near)]
    low, high = gate(low, high, *other)
    ahead_low, back_high = fetch(low, final(1)), fetch(high, final(-1))
    ahead_high, back_low = fetch(high, final(1)), fetch(low, final(-1))
    far_low, far_high = fetch(ahead_low, final(1)), fetch(back_high, final(-1))
    own = [low, high, ahead_low, ahead_high, back_low, back_high, far_low, far_high]
    other += [fetch(v, near) for v in own[2:]]

    rows, logits, stats, target = local_logits(ids, own, other, head)
    stats = merge(exchange(stats, ("z", "c")))
    stats = lax.all_to_all(stats, ("y", "x"), 0, 0, tiled=True)
    log_norm, weight, loss = preference(stats, lengths, ref_logps, pairing)

    logit_grad, send = grad_other_first(ids, logits, log_norm, weight, target, head)
    received = [fetch(send, near)]
    received.append(fetch(grad_other_second(ids, logit_grad, head), near))
    *parts, mark = grad_own(ids, logit_grad, head, received, arrived(received[0]))
    half, mark = grad_head_half(rows, logit_grad, mark)
    keep_low, keep_high, ahead_low, ahead_high, back_low, back_high, far_low, far_high = parts
    ahead_low, _ = add(ahead_low, fetch(far_low, final(-1)), mark)
    back_high, mark = add(back_high, fetch(far_high, final(1)), mark)
    grad_head, mark = grad_head_half(rows, logit_grad, mark, half)
    parts = split_middle(
        (keep_low, fetch(ahead_low, final(-1)), fetch(back_low, final(1))),
        (keep_high, fetch(ahead_high, final(-1)), fetch(back_high, final(1))),
        mark,
    )
    parts = split_window(parts[0], *(fetch(parts[s], middle(-OFF[s])) for s in (1, 2, 3)))
    grad_hidden = finish(lax.all_to_all(parts, ("z", "c"), 0, 0, tiled=True))
    return grad_hidden, grad_head, loss[0, 0]


def solution(mesh):
    fine = Mesh(mesh.devices.reshape(NY, NX, NZ, NC), AXES)
    return jax.shard_map(
        local,
        mesh=fine,
        in_specs=(P(AXES, None), P(None, AXES), P(AXES), P(AXES), P(), P(), P()),
        out_specs=(P(AXES, None), P(None, AXES), P()),
        check_vma=False,
    )
```

```python
import functools

import jax
import jax.numpy as jnp
from jax import lax
from jax.experimental import pallas as pl
from jax.experimental.pallas import tpu as pltpu
from jax.sharding import Mesh, PartitionSpec as P

V = 163840
CODES = 32768
WIN = 48
NEG = -1e30
BETA = 1.0
LOSS_SCALE = 4096.0

D = 4096
HALF = D // 2
COLS = 640
TOKENS = 768
META = 128
WIDE = HALF + META
NY, NX, NZ, NC = 4, 4, 8, 2
AXES = ("y", "x", "z", "c")
OFF = (0, 1, 3, 2)
bf16 = jnp.bfloat16
f32 = jnp.float32
VMEM = pl.BlockSpec(memory_space=pltpu.VMEM)
SMEM = pl.BlockSpec(memory_space=pltpu.SMEM)
HBM = pl.BlockSpec(memory_space=pltpu.HBM)
MB = 1024 * 1024
PIECE = HALF // 2


def flat(y, x, z, c):
    return ((y % NY * NX + x % NX) * NZ + z % NZ) * NC + c


def fetch(value, source):
    pairs = [
        (flat(*source(y, x, z, c)), flat(y, x, z, c))
        for y in range(NY) for x in range(NX) for z in range(NZ) for c in range(NC)
    ]
    return lax.ppermute(value, AXES, pairs)


def middle(step):
    return lambda y, x, z, c: (y + step, x, z, c) if c == 0 else (y, x + step, z, c)


def final(step):
    return lambda y, x, z, c: (y, x + step, z, c) if c == 0 else (y + step, x, z, c)


def near(y, x, z, c):
    return y, x, z, 1 - c


def window(ids, core, s, k):
    y, x = ids[0], ids[1]
    across = core == 0
    last = (jnp.where(across, x, y) + OFF[s]) % 4
    mid = (jnp.where(across, y, x) + OFF[k]) % 4
    return jnp.where(across, mid * NX + last, last * NX + mid)


def call(kernel, outs, ins, scratch=(), vmem=10, **cost):
    return pl.pallas_call(
        kernel,
        out_shape=outs,
        in_specs=ins,
        out_specs=jax.tree.map(lambda _: VMEM, outs),
        scratch_shapes=list(scratch),
        compiler_params=pltpu.CompilerParams(vmem_limit_bytes=vmem * MB),
        cost_estimate=pl.CostEstimate(
            flops=cost.get("flops", 0), bytes_accessed=cost.get("bytes_accessed", 0), transcendentals=0
        ),
    )


def shape(dims, dtype):
    return jax.ShapeDtypeStruct(dims, dtype)


def first_message_kernel(targets, hidden, out, tok):
    rows = hidden[...].astype(f32)
    row = lax.broadcasted_iota(jnp.int32, (16, 128), 0)
    lane = lax.broadcasted_iota(jnp.int32, (16, 128), 1)
    meta = jnp.zeros((16, 128), f32)
    for j in range(3):
        goal = targets[j]
        for n, digit in enumerate((goal & 255, (goal >> 8) & 255, goal >> 16)):
            meta = jnp.where((row == j) & (lane == n), digit.astype(f32), meta)
    meta = meta.astype(bf16)
    for half in range(2):
        for r in range(16):
            at = half * HALF + r * 128
            tok[pl.ds(r, 3, stride=16), :] = rows[:, at:at + 128]
        part = tok[...].astype(bf16)
        for z in range(NZ):
            out[2 * z + half, 0:48, :] = part
            out[2 * z + half, 48:64, :] = meta


def first_message(targets, hidden):
    return call(
        first_message_kernel, shape((16, 64, 128), bf16), [SMEM, VMEM], [pltpu.VMEM((48, 128), f32)]
    )(targets, hidden)


def join_window_kernel(ids, parts, out, tok, meta):
    for dev in range(16):
        tok[dev * 48:(dev + 1) * 48, :] = parts[dev, 0:48, :].astype(f32)
        meta[dev * 16:(dev + 1) * 16, :] = parts[dev, 48:64, :].astype(f32)
    for j in range(3):
        for r in range(16):
            out[j * 16:(j + 1) * 16, r * 128:(r + 1) * 128] = tok[pl.ds(j * 16 + r, 16, stride=48), :].astype(bf16)
        out[j * 16:(j + 1) * 16, HALF:WIDE] = meta[pl.ds(j, 16, stride=16), :].astype(bf16)


def join_window(ids, parts):
    return call(
        join_window_kernel,
        shape((WIN, WIDE), bf16),
        [SMEM, VMEM],
        [pltpu.VMEM((768, 128), f32), pltpu.VMEM((256, 128), f32)],
    )(ids, parts)


def join_blocks_kernel(a, b, c, d, after, low, high):
    low[0], low[1], high[0], high[1] = a[...], b[...], c[...], d[...]


def join_blocks(*blocks):
    return call(join_blocks_kernel, [shape((2, WIN, WIDE), bf16)] * 2, [VMEM] * 5)(*blocks)


def gate_kernel(low, high, first, second, out_low, out_high):
    out_low[...] = low[...]
    out_high[...] = high[...]


def gate(low, high, *marks):
    return call(gate_kernel, [shape(low.shape, low.dtype)] * 2, [VMEM] * 4)(low, high, *marks)


def columns_of(rows):
    full = jnp.concatenate([rows, jnp.zeros((128 - rows.shape[0], 128), f32)], axis=0)
    return full.T


def load_kernel(head_hbm, head, mark, sem):
    mark[...] = jnp.zeros_like(mark)
    copy = pltpu.make_async_copy(head_hbm, head, sem)
    copy.start()
    copy.wait()


def load_head(head):
    return call(
        load_kernel,
        (shape((D, COLS), bf16), shape((8, 128), f32)),
        [HBM],
        [pltpu.SemaphoreType.DMA],
        vmem=8,
        bytes_accessed=10 * MB,
    )(head)


def logits_kernel(
    ids, *refs
):
    own_blocks, other_blocks = refs[:8], refs[8:16]
    head, hidden, logits, stats, target, meta, cols = refs[16:]
    rows = 256
    core = ids[3]
    own = pl.multiple_of(core * HALF, HALF)
    oth = pl.multiple_of((1 - core) * HALF, HALF)
    for i, (a, b) in enumerate(zip(own_blocks, other_blocks)):
        for inner in range(2):
            s, k = i // 2, i % 2 * 2 + inner
            row = pl.multiple_of(window(ids, core, s, k) * WIN, 16)
            hidden[pl.ds(row, WIN), pl.ds(own, HALF)] = a[inner, :, 0:HALF]
            meta[pl.ds(row, WIN), :] = a[inner, :, HALF:WIDE].astype(f32)
            row = pl.multiple_of(window(ids, 1 - core, s, k) * WIN, 16)
            hidden[pl.ds(row, WIN), pl.ds(oth, HALF)] = b[inner, :, 0:HALF]
    first = ids[4] * COLS
    column = first + lax.broadcasted_iota(jnp.int32, (rows, COLS), 1)
    lane = lax.broadcasted_iota(jnp.int32, (rows, 128), 1)
    for i in range(TOKENS // rows):
        at = pl.ds(i * rows, rows)
        part = jnp.dot(hidden[at, :], head[...], preferred_element_type=f32)
        logits[at, :] = part
        digits = meta[at, :]
        goal = (digits[:, 0:1] + 256.0 * digits[:, 1:2] + 65536.0 * digits[:, 2:3]).astype(jnp.int32)
        in_range = (goal >= V - CODES) == (column >= V - CODES)
        masked = jnp.where(in_range, part, NEG)
        peak = jnp.max(masked, axis=1, keepdims=True)
        total = jnp.sum(jnp.where(in_range, jnp.exp(masked - peak), 0.0), axis=1, keepdims=True)
        hit = jnp.sum(jnp.where(column == goal, part, 0.0), axis=1, keepdims=True)
        norm = peak + jnp.log(jnp.maximum(total, 1e-37))
        cols[at, :] = jnp.where(lane == 0, norm, jnp.where(lane == 1, hit, goal.astype(f32)))
    stats[...] = jnp.zeros_like(stats)
    target[...] = jnp.zeros_like(target)
    for b in range(TOKENS // 128):
        turned = cols[b * 128:(b + 1) * 128, :].T
        for i in range(2):
            stats[i, b:b + 1, :] = turned[i:i + 1, :]
        target[b:b + 1, :] = turned[2:3, :]


def local_logits(ids, own, other, head):
    return pl.pallas_call(
        logits_kernel,
        out_shape=(
            shape((TOKENS, D), bf16),
            shape((TOKENS, COLS), f32),
            shape((2, 8, 128), f32),
            shape((8, 128), f32),
        ),
        in_specs=[SMEM] + [VMEM] * 17,
        out_specs=(VMEM, VMEM, VMEM, VMEM),
        scratch_shapes=[
            pltpu.VMEM((TOKENS, 128), f32),
            pltpu.VMEM((TOKENS, 128), f32),
        ],
        compiler_params=pltpu.CompilerParams(vmem_limit_bytes=25 * MB),
        cost_estimate=pl.CostEstimate(flops=2 * TOKENS * D * COLS, bytes_accessed=20 * MB, transcendentals=0),
    )(ids, *own, *other, head)


def exchange(value, axes):
    return lax.all_to_all(jnp.broadcast_to(value[None], (16,) + value.shape), axes, 0, 0, tiled=True)


def merged(parts):
    peak = parts[0, 0]
    for i in range(1, 16):
        peak = jnp.maximum(peak, parts[i, 0])
    total = jnp.zeros_like(peak)
    hit = jnp.zeros_like(peak)
    for i in range(16):
        total += jnp.exp(parts[i, 0] - peak)
        hit += parts[i, 1]
    return peak + jnp.log(total), hit


def merge_kernel(parts, out):
    norm, hit = merged(parts)
    for i in range(16):
        out[i, 0], out[i, 1] = norm, hit


def merge(parts):
    return call(merge_kernel, shape((16, 2, 8, 128), f32), [VMEM])(parts)


def preference_kernel(parts, lengths, ref_logps, pairing, norm, weight, loss):
    log_norm, hit = merged(parts)
    token_lp = hit - log_norm
    rows = lax.broadcasted_iota(jnp.int32, (8, 128), 0) * 128 + lax.broadcasted_iota(jnp.int32, (8, 128), 1)
    inner = rows % WIN
    group, position = rows // WIN, inner % 16 * 3 + inner // 16
    pairs = pairing.shape[0] // 2
    token_weight = jnp.zeros((8, 128), f32)
    losses = jnp.zeros((1, 1), f32)
    for k in range(pairs):
        sides = []
        for g in (pairing[2 * k], pairing[2 * k + 1]):
            count = lengths[g].astype(f32)
            live = (group == g) & (position < lengths[g])
            policy = jnp.sum(jnp.where(live, token_lp, 0.0), keepdims=True) / count
            sides.append((live, count, policy - ref_logps[g]))
        (live_c, count_c, chosen), (live_r, count_r, rejected) = sides
        margin = BETA * (chosen - rejected)
        losses += jnp.maximum(-margin, 0.0) + jnp.log1p(jnp.exp(-jnp.abs(margin)))
        pair_weight = -LOSS_SCALE * BETA * jax.nn.sigmoid(-margin) / pairs
        token_weight += jnp.where(live_c, pair_weight / count_c, 0.0)
        token_weight -= jnp.where(live_r, pair_weight / count_r, 0.0)
    norm[...] = log_norm
    weight[...] = token_weight
    loss[...] = jnp.broadcast_to(losses / pairs, (8, 128))


def preference(parts, lengths, ref_logps, pairing):
    return call(
        preference_kernel,
        [shape((8, 128), f32)] * 3,
        [VMEM, SMEM, SMEM, SMEM],
    )(parts, lengths, ref_logps, pairing)


BLOCK = 512
STEP = 256


def times_head(grad, rows):
    return lax.dot_general(grad, rows, (((1,), (1,)), ((), ())), preferred_element_type=f32)


def head_rows(half, start):
    return pl.ds(pl.multiple_of(half * HALF + start, STEP), STEP)


def other_piece(piece, ids, grad, head, out):
    for i in range(PIECE // STEP):
        rows = head[head_rows(1 - ids[3], piece * PIECE + i * STEP), :]
        out[:, i * STEP:(i + 1) * STEP] = times_head(grad[...], rows).astype(out.dtype)


def grad_other_first_kernel(ids, logits, norm, weight, target, head, grad, out):
    norm_c, weight_c, goal_c = columns_of(norm[...]), columns_of(weight[...]), columns_of(target[...])
    column = ids[4] * COLS + lax.broadcasted_iota(jnp.int32, (128, COLS), 1)
    for b in range(TOKENS // 128):
        goal = goal_c[:, b:b + 1].astype(jnp.int32)
        in_range = (goal >= V - CODES) == (column >= V - CODES)
        at = slice(b * 128, (b + 1) * 128)
        prob = jnp.exp(jnp.where(in_range, logits[at, :] - norm_c[:, b:b + 1], NEG))
        grad[at, :] = (weight_c[:, b:b + 1] * ((column == goal).astype(f32) - prob)).astype(bf16)
    other_piece(0, ids, grad, head, out)


def grad_other_first(ids, logits, norm, weight, target, head):
    return call(
        grad_other_first_kernel,
        (shape((TOKENS, COLS), bf16), shape((TOKENS, PIECE), bf16)),
        [SMEM] + [VMEM] * 5,
        vmem=16,
        flops=TOKENS * PIECE * COLS * 2,
        bytes_accessed=6 * MB,
    )(ids, logits, norm, weight, target, head)


def grad_other_second(ids, grad, head):
    return call(
        functools.partial(other_piece, 1),
        shape((TOKENS, PIECE), bf16),
        [SMEM, VMEM, VMEM],
        vmem=16,
        flops=TOKENS * PIECE * COLS * 4,
        bytes_accessed=16 * MB,
    )(ids, grad, head)


def arrived_kernel(value, mark):
    mark[...] = jnp.zeros_like(mark)


def arrived(value):
    return call(arrived_kernel, shape((8, 128), f32), [VMEM], vmem=4)(value)


def grad_own_kernel(ids, grad, head, out):
    for i in range(HALF // STEP):
        out[:, i * STEP:(i + 1) * STEP] = times_head(grad[...], head[head_rows(ids[3], i * STEP), :])


def grad_own(ids, grad, head):
    return call(
        grad_own_kernel,
        shape((TOKENS, HALF), f32),
        [SMEM, VMEM, VMEM],
        vmem=16,
        flops=TOKENS * HALF * COLS * 2,
        bytes_accessed=10 * MB,
    )(ids, grad, head)


PART_TYPES = (f32, f32, f32, bf16, bf16, f32, bf16, bf16)


def split_final_kernel(first, ids, own, other0, other1, after, *refs):
    parts, mark = refs[:-1], refs[-1]
    mark[...] = jnp.zeros_like(mark)
    for n, r in enumerate(parts, first):
        for inner in range(2):
            row = pl.multiple_of(window(ids, ids[3], n // 2, n % 2 * 2 + inner) * WIN, 16)
            for h, other in enumerate((other0, other1)):
                at = slice(h * PIECE, (h + 1) * PIECE)
                total = own[pl.ds(row, WIN), at] + other[pl.ds(row, WIN), :].astype(f32)
                r[inner, :, at] = total.astype(r.dtype)


def split_final(ids, own, other, after, first, last):
    return call(
        functools.partial(split_final_kernel, first),
        [shape((2, WIN, HALF), t) for t in PART_TYPES[first:last]] + [shape((8, 128), f32)],
        [SMEM] + [VMEM] * 4,
        vmem=18,
    )(ids, own, *other, after)


def head_kernel(hidden, grad, *refs):
    out, mark = refs[-2:]
    mark[...] = jnp.zeros_like(mark)
    out[...] = lax.dot_general(
        hidden[...], grad[...], (((0,), (0,)), ((), ())), preferred_element_type=f32
    ).astype(out.dtype)


def grad_head_half(hidden, grad, after, first=None):
    steps = D // BLOCK // 2
    base = 0 if first is None else steps
    return pl.pallas_call(
        head_kernel,
        grid=(steps,),
        in_specs=[
            pl.BlockSpec((TOKENS, BLOCK), lambda i: (0, i + base)),
            pl.BlockSpec((TOKENS, COLS), lambda i: (0, 0)),
            pl.BlockSpec((8, 128), lambda i: (0, 0)),
        ] + ([] if first is None else [pl.BlockSpec(memory_space=pl.ANY)]),
        out_specs=(pl.BlockSpec((BLOCK, COLS), lambda i: (i + base, 0)), pl.BlockSpec((8, 128), lambda i: (0, 0))),
        out_shape=(shape((D, COLS), bf16), shape((8, 128), f32)),
        input_output_aliases={} if first is None else {3: 0},
        compiler_params=pltpu.CompilerParams(vmem_limit_bytes=20 * MB),
        cost_estimate=pl.CostEstimate(flops=TOKENS * D * COLS, bytes_accessed=6 * MB, transcendentals=0),
    )(hidden, grad, after, *([] if first is None else [first]))


def add_four(a, b, c, d):
    return (a.astype(f32) + d.astype(f32)) + (b.astype(f32) + c.astype(f32))


def add_kernel(a, b, after, out, mark):
    mark[...] = jnp.zeros_like(mark)
    out[...] = (a[...] + b[...].astype(f32)).astype(out.dtype)


def add(a, b, after):
    return call(add_kernel, (shape(a.shape, bf16), shape((8, 128), f32)), [VMEM] * 3)(a, b, after)


def split_middle_kernel(*refs):
    ins, outs = refs[:6], refs[7:]
    for k, q in enumerate(outs):
        own, back, ahead = (ins[3 * (k // 2) + i][k % 2].astype(f32) for i in range(3))
        q[...] = (own + (back + ahead)).astype(q.dtype)


def split_middle(low, high, after):
    return call(
        split_middle_kernel,
        [shape((WIN, HALF), f32 if k == 0 else bf16) for k in range(4)],
        [VMEM] * 7,
        bytes_accessed=6 * MB,
    )(*low, *high, after)


def split_window_kernel(a, b, c, d, out, tok):
    total = add_four(a[...], b[...], c[...], d[...])
    for j in range(3):
        for r in range(16):
            tok[pl.ds(j * 16 + r, 16, stride=48), :] = total[j * 16:(j + 1) * 16, r * 128:(r + 1) * 128]
    for dev in range(16):
        out[dev] = tok[dev * 48:(dev + 1) * 48, :].astype(out.dtype)


def split_window(a, b, c, d):
    return call(
        split_window_kernel,
        shape((16, 48, 128), bf16),
        [VMEM] * 4,
        [pltpu.VMEM((768, 128), f32)],
    )(a, b, c, d)


def finish_kernel(parts, out, tok):
    for half in range(2):
        total = parts[half].astype(f32)
        for i in range(1, NZ):
            total += parts[2 * i + half].astype(f32)
        tok[...] = total
        for r in range(16):
            at = half * HALF + r * 128
            out[:, at:at + 128] = tok[pl.ds(r, 3, stride=16), :].astype(bf16)


def finish(parts):
    return call(finish_kernel, shape((3, D), bf16), [VMEM], [pltpu.VMEM((48, 128), f32)])(parts)


def local(hidden, head_weight, targets, image_mask, lengths, ref_logps, pairing):
    y, x, z, c = (lax.axis_index(a) for a in AXES)
    ids = jnp.stack([y, x, z, c, flat(y, x, z, c)]).astype(jnp.int32)

    parts = lax.all_to_all(first_message(targets, hidden), ("z", "c"), 0, 0, tiled=True)
    block = join_window(ids, parts)
    head, mark = load_head(head_weight)
    low, high = join_blocks(block, *(fetch(block, middle(o)) for o in OFF[1:]), mark)
    other = [fetch(low, near), fetch(high, near)]
    low, high = gate(low, high, *other)
    ahead_low, back_high = fetch(low, final(1)), fetch(high, final(-1))
    late_low, late_high = gate(low, high, ahead_low, back_high)
    ahead_high, back_low = fetch(late_high, final(1)), fetch(late_low, final(-1))
    far_low, far_high = fetch(ahead_low, final(1)), fetch(back_high, final(-1))
    own = [low, high, ahead_low, ahead_high, back_low, back_high, far_low, far_high]
    other += [fetch(v, near) for v in own[2:]]

    rows, logits, stats, target = local_logits(ids, own, other, head)
    stats = merge(exchange(stats, ("z", "c")))
    stats = lax.all_to_all(stats, ("y", "x"), 0, 0, tiled=True)
    log_norm, weight, loss = preference(stats, lengths, ref_logps, pairing)

    logit_grad, send = grad_other_first(ids, logits, log_norm, weight, target, head)
    received = [fetch(send, near)]
    received.append(fetch(grad_other_second(ids, logit_grad, head), near))
    own = grad_own(ids, logit_grad, head)
    far_low, far_high, mark = split_final(ids, own, received, arrived(received[0]), 6, 8)
    half, mark = grad_head_half(rows, logit_grad, mark)
    *parts, mark = split_final(ids, own, received, mark, 0, 6)
    keep_low, keep_high, ahead_low, ahead_high, back_low, back_high = parts
    ahead_low, _ = add(ahead_low, fetch(far_low, final(-1)), mark)
    back_high, mark = add(back_high, fetch(far_high, final(1)), mark)
    grad_head, mark = grad_head_half(rows, logit_grad, mark, half)
    parts = split_middle(
        (keep_low, fetch(ahead_low, final(-1)), fetch(back_low, final(1))),
        (keep_high, fetch(ahead_high, final(-1)), fetch(back_high, final(1))),
        mark,
    )
    parts = split_window(parts[0], *(fetch(parts[s], middle(-OFF[s])) for s in (1, 2, 3)))
    grad_hidden = finish(lax.all_to_all(parts, ("z", "c"), 0, 0, tiled=True))
    return grad_hidden, grad_head, loss[0, 0]


def solution(mesh):
    fine = Mesh(mesh.devices.reshape(NY, NX, NZ, NC), AXES)
    return jax.shard_map(
        local,
        mesh=fine,
        in_specs=(P(AXES, None), P(None, AXES), P(AXES), P(AXES), P(), P(), P()),
        out_specs=(P(AXES, None), P(None, AXES), P()),
        check_vma=False,
    )
```

```python
import functools

import jax
import jax.numpy as jnp
from jax import lax
from jax.experimental import pallas as pl
from jax.experimental.pallas import tpu as pltpu
from jax.sharding import Mesh, PartitionSpec as P

V = 163840
CODES = 32768
WIN = 48
NEG = -1e30
BETA = 1.0
LOSS_SCALE = 4096.0

D = 4096
HALF = D // 2
COLS = 640
TOKENS = 768
META = 128
WIDE = HALF + META
NY, NX, NZ, NC = 4, 4, 8, 2
AXES = ("y", "x", "z", "c")
OFF = (0, 1, 3, 2)
bf16 = jnp.bfloat16
f32 = jnp.float32
VMEM = pl.BlockSpec(memory_space=pltpu.VMEM)
SMEM = pl.BlockSpec(memory_space=pltpu.SMEM)
HBM = pl.BlockSpec(memory_space=pltpu.HBM)
MB = 1024 * 1024
PIECE = HALF // 2


def flat(y, x, z, c):
    return ((y % NY * NX + x % NX) * NZ + z % NZ) * NC + c


def fetch(value, source):
    pairs = [
        (flat(*source(y, x, z, c)), flat(y, x, z, c))
        for y in range(NY) for x in range(NX) for z in range(NZ) for c in range(NC)
    ]
    return lax.ppermute(value, AXES, pairs)


def middle(step):
    return lambda y, x, z, c: (y + step, x, z, c) if c == 0 else (y, x + step, z, c)


def final(step):
    return lambda y, x, z, c: (y, x + step, z, c) if c == 0 else (y + step, x, z, c)


def near(y, x, z, c):
    return y, x, z, 1 - c


def window(ids, core, s, k):
    y, x = ids[0], ids[1]
    across = core == 0
    last = (jnp.where(across, x, y) + OFF[s]) % 4
    mid = (jnp.where(across, y, x) + OFF[k]) % 4
    return jnp.where(across, mid * NX + last, last * NX + mid)


def call(kernel, outs, ins, scratch=(), vmem=10, **cost):
    return pl.pallas_call(
        kernel,
        out_shape=outs,
        in_specs=ins,
        out_specs=jax.tree.map(lambda _: VMEM, outs),
        scratch_shapes=list(scratch),
        compiler_params=pltpu.CompilerParams(vmem_limit_bytes=vmem * MB),
        cost_estimate=pl.CostEstimate(
            flops=cost.get("flops", 0), bytes_accessed=cost.get("bytes_accessed", 0), transcendentals=0
        ),
    )


def shape(dims, dtype):
    return jax.ShapeDtypeStruct(dims, dtype)


def first_message_kernel(targets, hidden, out, tok):
    rows = hidden[...].astype(f32)
    row = lax.broadcasted_iota(jnp.int32, (16, 128), 0)
    lane = lax.broadcasted_iota(jnp.int32, (16, 128), 1)
    meta = jnp.zeros((16, 128), f32)
    for j in range(3):
        goal = targets[j]
        for n, digit in enumerate((goal & 255, (goal >> 8) & 255, goal >> 16)):
            meta = jnp.where((row == j) & (lane == n), digit.astype(f32), meta)
    meta = meta.astype(bf16)
    for half in range(2):
        for r in range(16):
            at = half * HALF + r * 128
            tok[pl.ds(r, 3, stride=16), :] = rows[:, at:at + 128]
        part = tok[...].astype(bf16)
        for z in range(NZ):
            out[2 * z + half, 0:48, :] = part
            out[2 * z + half, 48:64, :] = meta


def first_message(targets, hidden):
    return call(
        first_message_kernel, shape((16, 64, 128), bf16), [SMEM, VMEM], [pltpu.VMEM((48, 128), f32)]
    )(targets, hidden)


def join_window_kernel(ids, parts, out, tok, meta):
    for dev in range(16):
        tok[dev * 48:(dev + 1) * 48, :] = parts[dev, 0:48, :].astype(f32)
        meta[dev * 16:(dev + 1) * 16, :] = parts[dev, 48:64, :].astype(f32)
    for j in range(3):
        for r in range(16):
            out[j * 16:(j + 1) * 16, r * 128:(r + 1) * 128] = tok[pl.ds(j * 16 + r, 16, stride=48), :].astype(bf16)
        out[j * 16:(j + 1) * 16, HALF:WIDE] = meta[pl.ds(j, 16, stride=16), :].astype(bf16)


def join_window(ids, parts):
    return call(
        join_window_kernel,
        shape((WIN, WIDE), bf16),
        [SMEM, VMEM],
        [pltpu.VMEM((768, 128), f32), pltpu.VMEM((256, 128), f32)],
    )(ids, parts)


def join_blocks_kernel(a, b, c, d, after, low, high):
    low[0], low[1], high[0], high[1] = a[...], b[...], c[...], d[...]


def join_blocks(*blocks):
    return call(join_blocks_kernel, [shape((2, WIN, WIDE), bf16)] * 2, [VMEM] * 5)(*blocks)


def gate_kernel(low, high, first, second, out_low, out_high):
    out_low[...] = low[...]
    out_high[...] = high[...]


def gate(low, high, *marks):
    return call(gate_kernel, [shape(low.shape, low.dtype)] * 2, [VMEM] * 4)(low, high, *marks)


def columns_of(rows):
    full = jnp.concatenate([rows, jnp.zeros((128 - rows.shape[0], 128), f32)], axis=0)
    return full.T


def load_kernel(head_hbm, head, mark, sem):
    mark[...] = jnp.zeros_like(mark)
    copy = pltpu.make_async_copy(head_hbm, head, sem)
    copy.start()
    copy.wait()


def load_head(head):
    return call(
        load_kernel,
        (shape((D, COLS), bf16), shape((8, 128), f32)),
        [HBM],
        [pltpu.SemaphoreType.DMA],
        vmem=8,
        bytes_accessed=10 * MB,
    )(head)


def logits_kernel(
    ids, *refs
):
    own_blocks, other_blocks = refs[:8], refs[8:16]
    head, hidden, logits, stats, target, meta, cols = refs[16:]
    rows = 256
    core = ids[3]
    own = pl.multiple_of(core * HALF, HALF)
    oth = pl.multiple_of((1 - core) * HALF, HALF)
    for i, (a, b) in enumerate(zip(own_blocks, other_blocks)):
        for inner in range(2):
            s, k = i // 2, i % 2 * 2 + inner
            row = pl.multiple_of(window(ids, core, s, k) * WIN, 16)
            hidden[pl.ds(row, WIN), pl.ds(own, HALF)] = a[inner, :, 0:HALF]
            meta[pl.ds(row, WIN), :] = a[inner, :, HALF:WIDE].astype(f32)
            row = pl.multiple_of(window(ids, 1 - core, s, k) * WIN, 16)
            hidden[pl.ds(row, WIN), pl.ds(oth, HALF)] = b[inner, :, 0:HALF]
    first = ids[4] * COLS
    column = first + lax.broadcasted_iota(jnp.int32, (rows, COLS), 1)
    lane = lax.broadcasted_iota(jnp.int32, (rows, 128), 1)
    for i in range(TOKENS // rows):
        at = pl.ds(i * rows, rows)
        part = jnp.dot(hidden[at, :], head[...], preferred_element_type=f32)
        logits[at, :] = part
        digits = meta[at, :]
        goal = (digits[:, 0:1] + 256.0 * digits[:, 1:2] + 65536.0 * digits[:, 2:3]).astype(jnp.int32)
        in_range = (goal >= V - CODES) == (column >= V - CODES)
        masked = jnp.where(in_range, part, NEG)
        peak = jnp.max(masked, axis=1, keepdims=True)
        total = jnp.sum(jnp.where(in_range, jnp.exp(masked - peak), 0.0), axis=1, keepdims=True)
        hit = jnp.sum(jnp.where(column == goal, part, 0.0), axis=1, keepdims=True)
        norm = peak + jnp.log(jnp.maximum(total, 1e-37))
        cols[at, :] = jnp.where(lane == 0, norm, jnp.where(lane == 1, hit, goal.astype(f32)))
    stats[...] = jnp.zeros_like(stats)
    target[...] = jnp.zeros_like(target)
    for b in range(TOKENS // 128):
        turned = cols[b * 128:(b + 1) * 128, :].T
        for i in range(2):
            stats[i, b:b + 1, :] = turned[i:i + 1, :]
        target[b:b + 1, :] = turned[2:3, :]


def local_logits(ids, own, other, head):
    return pl.pallas_call(
        logits_kernel,
        out_shape=(
            shape((TOKENS, D), bf16),
            shape((TOKENS, COLS), f32),
            shape((2, 8, 128), f32),
            shape((8, 128), f32),
        ),
        in_specs=[SMEM] + [VMEM] * 17,
        out_specs=(VMEM, VMEM, VMEM, VMEM),
        scratch_shapes=[
            pltpu.VMEM((TOKENS, 128), f32),
            pltpu.VMEM((TOKENS, 128), f32),
        ],
        compiler_params=pltpu.CompilerParams(vmem_limit_bytes=25 * MB),
        cost_estimate=pl.CostEstimate(flops=2 * TOKENS * D * COLS, bytes_accessed=20 * MB, transcendentals=0),
    )(ids, *own, *other, head)


def exchange(value, axes):
    return lax.all_to_all(jnp.broadcast_to(value[None], (16,) + value.shape), axes, 0, 0, tiled=True)


def merged(parts):
    peak = parts[0, 0]
    for i in range(1, 16):
        peak = jnp.maximum(peak, parts[i, 0])
    total = jnp.zeros_like(peak)
    hit = jnp.zeros_like(peak)
    for i in range(16):
        total += jnp.exp(parts[i, 0] - peak)
        hit += parts[i, 1]
    return peak + jnp.log(total), hit


def merge_kernel(parts, out):
    norm, hit = merged(parts)
    for i in range(16):
        out[i, 0], out[i, 1] = norm, hit


def merge(parts):
    return call(merge_kernel, shape((16, 2, 8, 128), f32), [VMEM])(parts)


def preference_kernel(parts, lengths, ref_logps, pairing, norm, weight, loss):
    log_norm, hit = merged(parts)
    token_lp = hit - log_norm
    rows = lax.broadcasted_iota(jnp.int32, (8, 128), 0) * 128 + lax.broadcasted_iota(jnp.int32, (8, 128), 1)
    inner = rows % WIN
    group, position = rows // WIN, inner % 16 * 3 + inner // 16
    pairs = pairing.shape[0] // 2
    token_weight = jnp.zeros((8, 128), f32)
    losses = jnp.zeros((1, 1), f32)
    for k in range(pairs):
        sides = []
        for g in (pairing[2 * k], pairing[2 * k + 1]):
            count = lengths[g].astype(f32)
            live = (group == g) & (position < lengths[g])
            policy = jnp.sum(jnp.where(live, token_lp, 0.0), keepdims=True) / count
            sides.append((live, count, policy - ref_logps[g]))
        (live_c, count_c, chosen), (live_r, count_r, rejected) = sides
        margin = BETA * (chosen - rejected)
        losses += jnp.maximum(-margin, 0.0) + jnp.log1p(jnp.exp(-jnp.abs(margin)))
        pair_weight = -LOSS_SCALE * BETA * jax.nn.sigmoid(-margin) / pairs
        token_weight += jnp.where(live_c, pair_weight / count_c, 0.0)
        token_weight -= jnp.where(live_r, pair_weight / count_r, 0.0)
    norm[...] = log_norm
    weight[...] = token_weight
    loss[...] = jnp.broadcast_to(losses / pairs, (8, 128))


def preference(parts, lengths, ref_logps, pairing):
    return call(
        preference_kernel,
        [shape((8, 128), f32)] * 3,
        [VMEM, SMEM, SMEM, SMEM],
    )(parts, lengths, ref_logps, pairing)


BLOCK = 512
STEP = 256


def times_head(grad, rows):
    return lax.dot_general(grad, rows, (((1,), (1,)), ((), ())), preferred_element_type=f32)


def head_rows(half, start):
    return pl.ds(pl.multiple_of(half * HALF + start, STEP), STEP)


def other_piece(piece, ids, grad, head, out):
    for i in range(PIECE // STEP):
        rows = head[head_rows(1 - ids[3], piece * PIECE + i * STEP), :]
        out[:, i * STEP:(i + 1) * STEP] = times_head(grad[...], rows).astype(out.dtype)


def grad_other_first_kernel(ids, logits, norm, weight, target, head, grad, out):
    norm_c, weight_c, goal_c = columns_of(norm[...]), columns_of(weight[...]), columns_of(target[...])
    column = ids[4] * COLS + lax.broadcasted_iota(jnp.int32, (128, COLS), 1)
    for b in range(TOKENS // 128):
        goal = goal_c[:, b:b + 1].astype(jnp.int32)
        in_range = (goal >= V - CODES) == (column >= V - CODES)
        at = slice(b * 128, (b + 1) * 128)
        prob = jnp.exp(jnp.where(in_range, logits[at, :] - norm_c[:, b:b + 1], NEG))
        grad[at, :] = (weight_c[:, b:b + 1] * ((column == goal).astype(f32) - prob)).astype(bf16)
    other_piece(0, ids, grad, head, out)


def grad_other_first(ids, logits, norm, weight, target, head):
    return call(
        grad_other_first_kernel,
        (shape((TOKENS, COLS), bf16), shape((TOKENS, PIECE), bf16)),
        [SMEM] + [VMEM] * 5,
        vmem=16,
        flops=TOKENS * PIECE * COLS * 2,
        bytes_accessed=6 * MB,
    )(ids, logits, norm, weight, target, head)


def grad_other_second(ids, grad, head):
    return call(
        functools.partial(other_piece, 1),
        shape((TOKENS, PIECE), bf16),
        [SMEM, VMEM, VMEM],
        vmem=16,
        flops=TOKENS * PIECE * COLS * 4,
        bytes_accessed=16 * MB,
    )(ids, grad, head)


def arrived_kernel(value, mark):
    mark[...] = jnp.zeros_like(mark)


def arrived(value):
    return call(arrived_kernel, shape((8, 128), f32), [VMEM], vmem=4)(value)


def grad_own_kernel(ids, grad, head, out):
    for i in range(HALF // STEP):
        out[:, i * STEP:(i + 1) * STEP] = times_head(grad[...], head[head_rows(ids[3], i * STEP), :])


def grad_own(ids, grad, head):
    return call(
        grad_own_kernel,
        shape((TOKENS, HALF), f32),
        [SMEM, VMEM, VMEM],
        vmem=16,
        flops=TOKENS * HALF * COLS * 2,
        bytes_accessed=10 * MB,
    )(ids, grad, head)


PART_TYPES = (f32, f32, f32, bf16, bf16, f32, bf16, bf16)


def split_final_kernel(first, ids, own, other0, other1, after, *refs):
    parts, mark = refs[:-1], refs[-1]
    mark[...] = jnp.zeros_like(mark)
    for n, r in enumerate(parts, first):
        for inner in range(2):
            row = pl.multiple_of(window(ids, ids[3], n // 2, n % 2 * 2 + inner) * WIN, 16)
            for h, other in enumerate((other0, other1)):
                at = slice(h * PIECE, (h + 1) * PIECE)
                total = own[pl.ds(row, WIN), at] + other[pl.ds(row, WIN), :].astype(f32)
                r[inner, :, at] = total.astype(r.dtype)


def split_final(ids, own, other, after, first, last):
    return call(
        functools.partial(split_final_kernel, first),
        [shape((2, WIN, HALF), t) for t in PART_TYPES[first:last]] + [shape((8, 128), f32)],
        [SMEM] + [VMEM] * 4,
        vmem=18,
    )(ids, own, *other, after)


def head_kernel(hidden, grad, *refs):
    out, mark = refs[-2:]
    mark[...] = jnp.zeros_like(mark)
    out[...] = lax.dot_general(
        hidden[...], grad[...], (((0,), (0,)), ((), ())), preferred_element_type=f32
    ).astype(out.dtype)


def grad_head_half(hidden, grad, after, first=None):
    steps = D // BLOCK // 2
    base = 0 if first is None else steps
    return pl.pallas_call(
        head_kernel,
        grid=(steps,),
        in_specs=[
            pl.BlockSpec((TOKENS, BLOCK), lambda i: (0, i + base)),
            pl.BlockSpec((TOKENS, COLS), lambda i: (0, 0)),
            pl.BlockSpec((8, 128), lambda i: (0, 0)),
        ] + ([] if first is None else [pl.BlockSpec(memory_space=pl.ANY)]),
        out_specs=(pl.BlockSpec((BLOCK, COLS), lambda i: (i + base, 0)), pl.BlockSpec((8, 128), lambda i: (0, 0))),
        out_shape=(shape((D, COLS), bf16), shape((8, 128), f32)),
        input_output_aliases={} if first is None else {3: 0},
        compiler_params=pltpu.CompilerParams(vmem_limit_bytes=20 * MB),
        cost_estimate=pl.CostEstimate(flops=TOKENS * D * COLS, bytes_accessed=6 * MB, transcendentals=0),
    )(hidden, grad, after, *([] if first is None else [first]))


def add_four(a, b, c, d):
    return (a.astype(f32) + d.astype(f32)) + (b.astype(f32) + c.astype(f32))


def add_kernel(a, b, after, out, mark):
    mark[...] = jnp.zeros_like(mark)
    out[...] = (a[...] + b[...].astype(f32)).astype(out.dtype)


def add(a, b, after):
    return call(add_kernel, (shape(a.shape, bf16), shape((8, 128), f32)), [VMEM] * 3)(a, b, after)


def split_middle_kernel(*refs):
    ins, outs = refs[:6], refs[7:]
    for k, q in enumerate(outs):
        own, back, ahead = (ins[3 * (k // 2) + i][k % 2].astype(f32) for i in range(3))
        q[...] = (own + (back + ahead)).astype(q.dtype)


def split_middle(low, high, after):
    return call(
        split_middle_kernel,
        [shape((WIN, HALF), f32 if k == 0 else bf16) for k in range(4)],
        [VMEM] * 7,
        bytes_accessed=6 * MB,
    )(*low, *high, after)


def split_window_kernel(a, b, c, d, out, tok):
    total = add_four(a[...], b[...], c[...], d[...])
    for j in range(3):
        for r in range(16):
            tok[pl.ds(j * 16 + r, 16, stride=48), :] = total[j * 16:(j + 1) * 16, r * 128:(r + 1) * 128]
    for dev in range(16):
        out[dev] = tok[dev * 48:(dev + 1) * 48, :].astype(out.dtype)


def split_window(a, b, c, d):
    return call(
        split_window_kernel,
        shape((16, 48, 128), bf16),
        [VMEM] * 4,
        [pltpu.VMEM((768, 128), f32)],
    )(a, b, c, d)


def finish_kernel(parts, out, tok):
    for half in range(2):
        total = parts[half].astype(f32)
        for i in range(1, NZ):
            total += parts[2 * i + half].astype(f32)
        tok[...] = total
        for r in range(16):
            at = half * HALF + r * 128
            out[:, at:at + 128] = tok[pl.ds(r, 3, stride=16), :].astype(bf16)


def finish(parts):
    return call(finish_kernel, shape((3, D), bf16), [VMEM], [pltpu.VMEM((48, 128), f32)])(parts)


def local(hidden, head_weight, targets, image_mask, lengths, ref_logps, pairing):
    y, x, z, c = (lax.axis_index(a) for a in AXES)
    ids = jnp.stack([y, x, z, c, flat(y, x, z, c)]).astype(jnp.int32)

    parts = lax.all_to_all(first_message(targets, hidden), ("z", "c"), 0, 0, tiled=True)
    block = join_window(ids, parts)
    head, mark = load_head(head_weight)
    low, high = join_blocks(block, *(fetch(block, middle(o)) for o in OFF[1:]), mark)
    other = [fetch(low, near), fetch(high, near)]
    low, high = gate(low, high, *other)
    ahead_low, back_high = fetch(low, final(1)), fetch(high, final(-1))
    ahead_high, back_low = fetch(high, final(1)), fetch(low, final(-1))
    far_low, far_high = fetch(ahead_low, final(1)), fetch(back_high, final(-1))
    own = [low, high, ahead_low, ahead_high, back_low, back_high, far_low, far_high]
    other += [fetch(v, near) for v in own[2:]]

    rows, logits, stats, target = local_logits(ids, own, other, head)
    stats = merge(exchange(stats, ("z", "c")))
    stats = lax.all_to_all(stats, ("y", "x"), 0, 0, tiled=True)
    log_norm, weight, loss = preference(stats, lengths, ref_logps, pairing)

    logit_grad, send = grad_other_first(ids, logits, log_norm, weight, target, head)
    received = [fetch(send, near)]
    received.append(fetch(grad_other_second(ids, logit_grad, head), near))
    own = grad_own(ids, logit_grad, head)
    *parts, mark = split_final(ids, own, received, arrived(received[0]), 0, 8)
    keep_low, keep_high, ahead_low, ahead_high, back_low, back_high, far_low, far_high = parts
    half, mark = grad_head_half(rows, logit_grad, mark)
    ahead_low, _ = add(ahead_low, fetch(far_low, final(-1)), mark)
    back_high, mark = add(back_high, fetch(far_high, final(1)), mark)
    grad_head, mark = grad_head_half(rows, logit_grad, mark, half)
    parts = split_middle(
        (keep_low, fetch(ahead_low, final(-1)), fetch(back_low, final(1))),
        (keep_high, fetch(ahead_high, final(-1)), fetch(back_high, final(1))),
        mark,
    )
    parts = split_window(parts[0], *(fetch(parts[s], middle(-OFF[s])) for s in (1, 2, 3)))
    grad_hidden = finish(lax.all_to_all(parts, ("z", "c"), 0, 0, tiled=True))
    return grad_hidden, grad_head, loss[0, 0]


def solution(mesh):
    fine = Mesh(mesh.devices.reshape(NY, NX, NZ, NC), AXES)
    return jax.shard_map(
        local,
        mesh=fine,
        in_specs=(P(AXES, None), P(None, AXES), P(AXES), P(AXES), P(), P(), P()),
        out_specs=(P(AXES, None), P(None, AXES), P()),
        check_vma=False,
    )
```

```python
import functools

import jax
import jax.numpy as jnp
from jax import lax
from jax.experimental import pallas as pl
from jax.experimental.pallas import tpu as pltpu
from jax.sharding import Mesh, PartitionSpec as P

V = 163840
CODES = 32768
WIN = 48
NEG = -1e30
BETA = 1.0
LOSS_SCALE = 4096.0

D = 4096
HALF = D // 2
COLS = 640
TOKENS = 768
META = 128
WIDE = HALF + META
NY, NX, NZ, NC = 4, 4, 8, 2
AXES = ("y", "x", "z", "c")
OFF = (0, 1, 3, 2)
bf16 = jnp.bfloat16
f32 = jnp.float32
VMEM = pl.BlockSpec(memory_space=pltpu.VMEM)
SMEM = pl.BlockSpec(memory_space=pltpu.SMEM)
HBM = pl.BlockSpec(memory_space=pltpu.HBM)
MB = 1024 * 1024
PIECE = HALF // 2


def flat(y, x, z, c):
    return ((y % NY * NX + x % NX) * NZ + z % NZ) * NC + c


def fetch(value, source):
    pairs = [
        (flat(*source(y, x, z, c)), flat(y, x, z, c))
        for y in range(NY) for x in range(NX) for z in range(NZ) for c in range(NC)
    ]
    return lax.ppermute(value, AXES, pairs)


def middle(step):
    return lambda y, x, z, c: (y + step, x, z, c) if c == 0 else (y, x + step, z, c)


def final(step):
    return lambda y, x, z, c: (y, x + step, z, c) if c == 0 else (y + step, x, z, c)


def near(y, x, z, c):
    return y, x, z, 1 - c


def window(ids, core, s, k):
    y, x = ids[0], ids[1]
    across = core == 0
    last = (jnp.where(across, x, y) + OFF[s]) % 4
    mid = (jnp.where(across, y, x) + OFF[k]) % 4
    return jnp.where(across, mid * NX + last, last * NX + mid)


def call(kernel, outs, ins, scratch=(), vmem=10, **cost):
    return pl.pallas_call(
        kernel,
        out_shape=outs,
        in_specs=ins,
        out_specs=jax.tree.map(lambda _: VMEM, outs),
        scratch_shapes=list(scratch),
        compiler_params=pltpu.CompilerParams(vmem_limit_bytes=vmem * MB),
        cost_estimate=pl.CostEstimate(
            flops=cost.get("flops", 0), bytes_accessed=cost.get("bytes_accessed", 0), transcendentals=0
        ),
    )


def shape(dims, dtype):
    return jax.ShapeDtypeStruct(dims, dtype)


def first_message_kernel(targets, hidden, out, tok):
    rows = hidden[...].astype(f32)
    row = lax.broadcasted_iota(jnp.int32, (16, 128), 0)
    lane = lax.broadcasted_iota(jnp.int32, (16, 128), 1)
    meta = jnp.zeros((16, 128), f32)
    for j in range(3):
        goal = targets[j]
        for n, digit in enumerate((goal & 255, (goal >> 8) & 255, goal >> 16)):
            meta = jnp.where((row == j) & (lane == n), digit.astype(f32), meta)
    meta = meta.astype(bf16)
    for half in range(2):
        for r in range(16):
            at = half * HALF + r * 128
            tok[pl.ds(r, 3, stride=16), :] = rows[:, at:at + 128]
        part = tok[...].astype(bf16)
        for z in range(NZ):
            out[2 * z + half, 0:48, :] = part
            out[2 * z + half, 48:64, :] = meta


def first_message(targets, hidden):
    return call(
        first_message_kernel, shape((16, 64, 128), bf16), [SMEM, VMEM], [pltpu.VMEM((48, 128), f32)], vmem=56
    )(targets, hidden)


def join_window_kernel(ids, parts, out, tok, meta):
    for dev in range(16):
        tok[dev * 48:(dev + 1) * 48, :] = parts[dev, 0:48, :].astype(f32)
        meta[dev * 16:(dev + 1) * 16, :] = parts[dev, 48:64, :].astype(f32)
    for j in range(3):
        for r in range(16):
            out[j * 16:(j + 1) * 16, r * 128:(r + 1) * 128] = tok[pl.ds(j * 16 + r, 16, stride=48), :].astype(bf16)
        out[j * 16:(j + 1) * 16, HALF:WIDE] = meta[pl.ds(j, 16, stride=16), :].astype(bf16)


def join_window(ids, parts):
    return call(
        join_window_kernel,
        shape((WIN, WIDE), bf16),
        [SMEM, VMEM],
        [pltpu.VMEM((768, 128), f32), pltpu.VMEM((256, 128), f32)],
    )(ids, parts)


def join_blocks_kernel(a, b, c, d, after, low, high, mark):
    mark[...] = jnp.zeros_like(mark)
    low[0], low[1], high[0], high[1] = a[...], b[...], c[...], d[...]


def join_blocks(*blocks):
    outs = [shape((2, WIN, WIDE), bf16)] * 2 + [shape((8, 128), f32)]
    return call(join_blocks_kernel, outs, [VMEM] * 5)(*blocks)


def gate_kernel(low, high, after, out_low, out_high):
    out_low[...] = low[...]
    out_high[...] = high[...]


def gate(low, high, after):
    return call(gate_kernel, [shape(low.shape, low.dtype)] * 2, [VMEM] * 3)(low, high, after)


def columns_of(rows):
    full = jnp.concatenate([rows, jnp.zeros((128 - rows.shape[0], 128), f32)], axis=0)
    return full.T


def load_kernel(head_hbm, head, mark, sem):
    mark[...] = jnp.zeros_like(mark)
    copy = pltpu.make_async_copy(head_hbm, head, sem)
    copy.start()
    copy.wait()


def load_head(head):
    return call(
        load_kernel,
        (shape((D, COLS), bf16), shape((8, 128), f32)),
        [HBM],
        [pltpu.SemaphoreType.DMA],
        vmem=8,
        bytes_accessed=10 * MB,
    )(head)


def logits_kernel(
    ids, *refs
):
    own_blocks, other_blocks = refs[:8], refs[8:16]
    head, hidden, logits, stats, target, meta, cols = refs[16:]
    rows = 256
    core = ids[3]
    own = pl.multiple_of(core * HALF, HALF)
    oth = pl.multiple_of((1 - core) * HALF, HALF)
    for i, (a, b) in enumerate(zip(own_blocks, other_blocks)):
        for inner in range(2):
            s, k = i // 2, i % 2 * 2 + inner
            row = pl.multiple_of(window(ids, core, s, k) * WIN, 16)
            hidden[pl.ds(row, WIN), pl.ds(own, HALF)] = a[inner, :, 0:HALF]
            meta[pl.ds(row, WIN), :] = a[inner, :, HALF:WIDE].astype(f32)
            row = pl.multiple_of(window(ids, 1 - core, s, k) * WIN, 16)
            hidden[pl.ds(row, WIN), pl.ds(oth, HALF)] = b[inner, :, 0:HALF]
    first = ids[4] * COLS
    column = first + lax.broadcasted_iota(jnp.int32, (rows, COLS), 1)
    lane = lax.broadcasted_iota(jnp.int32, (rows, 128), 1)
    for i in range(TOKENS // rows):
        at = pl.ds(i * rows, rows)
        part = jnp.dot(hidden[at, :], head[...], preferred_element_type=f32)
        logits[at, :] = part
        digits = meta[at, :]
        goal = (digits[:, 0:1] + 256.0 * digits[:, 1:2] + 65536.0 * digits[:, 2:3]).astype(jnp.int32)
        in_range = (goal >= V - CODES) == (column >= V - CODES)
        masked = jnp.where(in_range, part, NEG)
        peak = jnp.max(masked, axis=1, keepdims=True)
        total = jnp.sum(jnp.where(in_range, jnp.exp(masked - peak), 0.0), axis=1, keepdims=True)
        hit = jnp.sum(jnp.where(column == goal, part, 0.0), axis=1, keepdims=True)
        norm = peak + jnp.log(jnp.maximum(total, 1e-37))
        cols[at, :] = jnp.where(lane == 0, norm, jnp.where(lane == 1, hit, goal.astype(f32)))
    stats[...] = jnp.zeros_like(stats)
    target[...] = jnp.zeros_like(target)
    for b in range(TOKENS // 128):
        turned = cols[b * 128:(b + 1) * 128, :].T
        for i in range(2):
            stats[i, b:b + 1, :] = turned[i:i + 1, :]
        target[b:b + 1, :] = turned[2:3, :]


def local_logits(ids, own, other, head):
    return pl.pallas_call(
        logits_kernel,
        out_shape=(
            shape((TOKENS, D), bf16),
            shape((TOKENS, COLS), f32),
            shape((2, 8, 128), f32),
            shape((8, 128), f32),
        ),
        in_specs=[SMEM] + [VMEM] * 17,
        out_specs=(VMEM, VMEM, VMEM, VMEM),
        scratch_shapes=[
            pltpu.VMEM((TOKENS, 128), f32),
            pltpu.VMEM((TOKENS, 128), f32),
        ],
        compiler_params=pltpu.CompilerParams(vmem_limit_bytes=25 * MB),
        cost_estimate=pl.CostEstimate(flops=2 * TOKENS * D * COLS, bytes_accessed=20 * MB, transcendentals=0),
    )(ids, *own, *other, head)


def exchange(value, axes):
    return lax.all_to_all(jnp.broadcast_to(value[None], (16,) + value.shape), axes, 0, 0, tiled=True)


def merged(parts):
    peak = parts[0, 0]
    for i in range(1, 16):
        peak = jnp.maximum(peak, parts[i, 0])
    total = jnp.zeros_like(peak)
    hit = jnp.zeros_like(peak)
    for i in range(16):
        total += jnp.exp(parts[i, 0] - peak)
        hit += parts[i, 1]
    return peak + jnp.log(total), hit


def merge_kernel(parts, out):
    norm, hit = merged(parts)
    for i in range(16):
        out[i, 0], out[i, 1] = norm, hit


def merge(parts):
    return call(merge_kernel, shape((16, 2, 8, 128), f32), [VMEM])(parts)


def preference_kernel(parts, lengths, ref_logps, pairing, norm, weight, loss):
    log_norm, hit = merged(parts)
    token_lp = hit - log_norm
    rows = lax.broadcasted_iota(jnp.int32, (8, 128), 0) * 128 + lax.broadcasted_iota(jnp.int32, (8, 128), 1)
    inner = rows % WIN
    group, position = rows // WIN, inner % 16 * 3 + inner // 16
    pairs = pairing.shape[0] // 2
    token_weight = jnp.zeros((8, 128), f32)
    losses = jnp.zeros((1, 1), f32)
    for k in range(pairs):
        sides = []
        for g in (pairing[2 * k], pairing[2 * k + 1]):
            count = lengths[g].astype(f32)
            live = (group == g) & (position < lengths[g])
            policy = jnp.sum(jnp.where(live, token_lp, 0.0), keepdims=True) / count
            sides.append((live, count, policy - ref_logps[g]))
        (live_c, count_c, chosen), (live_r, count_r, rejected) = sides
        margin = BETA * (chosen - rejected)
        losses += jnp.maximum(-margin, 0.0) + jnp.log1p(jnp.exp(-jnp.abs(margin)))
        pair_weight = -LOSS_SCALE * BETA * jax.nn.sigmoid(-margin) / pairs
        token_weight += jnp.where(live_c, pair_weight / count_c, 0.0)
        token_weight -= jnp.where(live_r, pair_weight / count_r, 0.0)
    norm[...] = log_norm
    weight[...] = token_weight
    loss[...] = jnp.broadcast_to(losses / pairs, (8, 128))


def preference(parts, lengths, ref_logps, pairing):
    return call(
        preference_kernel,
        [shape((8, 128), f32)] * 3,
        [VMEM, SMEM, SMEM, SMEM],
    )(parts, lengths, ref_logps, pairing)


BLOCK = 512
STEP = 256


def times_head(grad, rows):
    return lax.dot_general(grad, rows, (((1,), (1,)), ((), ())), preferred_element_type=f32)


def head_rows(half, start):
    return pl.ds(pl.multiple_of(half * HALF + start, STEP), STEP)


def other_piece(piece, ids, grad, head, out):
    for i in range(PIECE // STEP):
        rows = head[head_rows(1 - ids[3], piece * PIECE + i * STEP), :]
        out[:, i * STEP:(i + 1) * STEP] = times_head(grad[...], rows).astype(out.dtype)


def grad_other_first_kernel(ids, logits, norm, weight, target, head, grad, out):
    norm_c, weight_c, goal_c = columns_of(norm[...]), columns_of(weight[...]), columns_of(target[...])
    column = ids[4] * COLS + lax.broadcasted_iota(jnp.int32, (128, COLS), 1)
    for b in range(TOKENS // 128):
        goal = goal_c[:, b:b + 1].astype(jnp.int32)
        in_range = (goal >= V - CODES) == (column >= V - CODES)
        at = slice(b * 128, (b + 1) * 128)
        prob = jnp.exp(jnp.where(in_range, logits[at, :] - norm_c[:, b:b + 1], NEG))
        grad[at, :] = (weight_c[:, b:b + 1] * ((column == goal).astype(f32) - prob)).astype(bf16)
    other_piece(0, ids, grad, head, out)


def grad_other_first(ids, logits, norm, weight, target, head):
    return call(
        grad_other_first_kernel,
        (shape((TOKENS, COLS), bf16), shape((TOKENS, PIECE), bf16)),
        [SMEM] + [VMEM] * 5,
        vmem=16,
        flops=TOKENS * PIECE * COLS * 2,
        bytes_accessed=6 * MB,
    )(ids, logits, norm, weight, target, head)


def grad_other_second(ids, grad, head):
    return call(
        functools.partial(other_piece, 1),
        shape((TOKENS, PIECE), bf16),
        [SMEM, VMEM, VMEM],
        vmem=16,
        flops=TOKENS * PIECE * COLS * 4,
        bytes_accessed=16 * MB,
    )(ids, grad, head)


def arrived_kernel(value, mark):
    mark[...] = jnp.zeros_like(mark)


def arrived(value):
    return call(arrived_kernel, shape((8, 128), f32), [VMEM], vmem=4)(value)


def grad_own_kernel(ids, grad, head, out):
    for i in range(HALF // STEP):
        out[:, i * STEP:(i + 1) * STEP] = times_head(grad[...], head[head_rows(ids[3], i * STEP), :])


def grad_own(ids, grad, head):
    return call(
        grad_own_kernel,
        shape((TOKENS, HALF), f32),
        [SMEM, VMEM, VMEM],
        vmem=16,
        flops=TOKENS * HALF * COLS * 2,
        bytes_accessed=10 * MB,
    )(ids, grad, head)


PART_TYPES = (f32, f32, f32, bf16, bf16, f32, bf16, bf16)


def split_final_kernel(first, ids, own, other0, other1, after, *refs):
    parts, mark = refs[:-1], refs[-1]
    mark[...] = jnp.zeros_like(mark)
    for n, r in enumerate(parts, first):
        for inner in range(2):
            row = pl.multiple_of(window(ids, ids[3], n // 2, n % 2 * 2 + inner) * WIN, 16)
            for h, other in enumerate((other0, other1)):
                at = slice(h * PIECE, (h + 1) * PIECE)
                total = own[pl.ds(row, WIN), at] + other[pl.ds(row, WIN), :].astype(f32)
                r[inner, :, at] = total.astype(r.dtype)


def split_final(ids, own, other, after, first, last):
    return call(
        functools.partial(split_final_kernel, first),
        [shape((2, WIN, HALF), t) for t in PART_TYPES[first:last]] + [shape((8, 128), f32)],
        [SMEM] + [VMEM] * 4,
        vmem=18,
    )(ids, own, *other, after)


def head_kernel(hidden, grad, *refs):
    out, mark = refs[-2:]
    mark[...] = jnp.zeros_like(mark)
    out[...] = lax.dot_general(
        hidden[...], grad[...], (((0,), (0,)), ((), ())), preferred_element_type=f32
    ).astype(out.dtype)


def grad_head_half(hidden, grad, after, first=None):
    steps = D // BLOCK // 2
    base = 0 if first is None else steps
    return pl.pallas_call(
        head_kernel,
        grid=(steps,),
        in_specs=[
            pl.BlockSpec((TOKENS, BLOCK), lambda i: (0, i + base)),
            pl.BlockSpec((TOKENS, COLS), lambda i: (0, 0)),
            pl.BlockSpec((8, 128), lambda i: (0, 0)),
        ] + ([] if first is None else [pl.BlockSpec(memory_space=pl.ANY)]),
        out_specs=(pl.BlockSpec((BLOCK, COLS), lambda i: (i + base, 0)), pl.BlockSpec((8, 128), lambda i: (0, 0))),
        out_shape=(shape((D, COLS), bf16), shape((8, 128), f32)),
        input_output_aliases={} if first is None else {3: 0},
        compiler_params=pltpu.CompilerParams(vmem_limit_bytes=20 * MB),
        cost_estimate=pl.CostEstimate(flops=TOKENS * D * COLS, bytes_accessed=6 * MB, transcendentals=0),
    )(hidden, grad, after, *([] if first is None else [first]))


def add_four(a, b, c, d):
    return (a.astype(f32) + d.astype(f32)) + (b.astype(f32) + c.astype(f32))


def add_kernel(a, b, after, out, mark):
    mark[...] = jnp.zeros_like(mark)
    out[...] = (a[...] + b[...].astype(f32)).astype(out.dtype)


def add(a, b, after):
    return call(add_kernel, (shape(a.shape, bf16), shape((8, 128), f32)), [VMEM] * 3)(a, b, after)


def split_middle_kernel(*refs):
    ins, outs = refs[:6], refs[7:]
    for k, q in enumerate(outs):
        own, back, ahead = (ins[3 * (k // 2) + i][k % 2].astype(f32) for i in range(3))
        q[...] = (own + (back + ahead)).astype(q.dtype)


def split_middle(low, high, after):
    return call(
        split_middle_kernel,
        [shape((WIN, HALF), f32 if k == 0 else bf16) for k in range(4)],
        [VMEM] * 7,
        bytes_accessed=6 * MB,
    )(*low, *high, after)


def split_window_kernel(a, b, c, d, out, tok):
    total = add_four(a[...], b[...], c[...], d[...])
    for j in range(3):
        for r in range(16):
            tok[pl.ds(j * 16 + r, 16, stride=48), :] = total[j * 16:(j + 1) * 16, r * 128:(r + 1) * 128]
    for dev in range(16):
        out[dev] = tok[dev * 48:(dev + 1) * 48, :].astype(out.dtype)


def split_window(a, b, c, d):
    return call(
        split_window_kernel,
        shape((16, 48, 128), bf16),
        [VMEM] * 4,
        [pltpu.VMEM((768, 128), f32)],
    )(a, b, c, d)


def finish_kernel(parts, out, tok):
    for half in range(2):
        total = parts[half].astype(f32)
        for i in range(1, NZ):
            total += parts[2 * i + half].astype(f32)
        tok[...] = total
        for r in range(16):
            at = half * HALF + r * 128
            out[:, at:at + 128] = tok[pl.ds(r, 3, stride=16), :].astype(bf16)


def finish(parts):
    return call(finish_kernel, shape((3, D), bf16), [VMEM], [pltpu.VMEM((48, 128), f32)])(parts)


def local(hidden, head_weight, targets, image_mask, lengths, ref_logps, pairing):
    y, x, z, c = (lax.axis_index(a) for a in AXES)
    ids = jnp.stack([y, x, z, c, flat(y, x, z, c)]).astype(jnp.int32)

    parts = lax.all_to_all(first_message(targets, hidden), ("z", "c"), 0, 0, tiled=True)
    block = join_window(ids, parts)
    head, mark = load_head(head_weight)
    low, high, mark = join_blocks(block, *(fetch(block, middle(o)) for o in OFF[1:]), mark)
    low, high = gate(low, high, fetch(mark, near))
    ahead_low, back_high = fetch(low, final(1)), fetch(high, final(-1))
    ahead_high, back_low = fetch(high, final(1)), fetch(low, final(-1))
    far_low, far_high = fetch(ahead_low, final(1)), fetch(back_high, final(-1))
    own = [low, high, ahead_low, ahead_high, back_low, back_high, far_low, far_high]
    other = [fetch(v, near) for v in own]

    rows, logits, stats, target = local_logits(ids, own, other, head)
    stats = merge(exchange(stats, ("z", "c")))
    stats = lax.all_to_all(stats, ("y", "x"), 0, 0, tiled=True)
    log_norm, weight, loss = preference(stats, lengths, ref_logps, pairing)

    logit_grad, send = grad_other_first(ids, logits, log_norm, weight, target, head)
    received = [fetch(send, near)]
    received.append(fetch(grad_other_second(ids, logit_grad, head), near))
    own = grad_own(ids, logit_grad, head)
    *parts, mark = split_final(ids, own, received, arrived(received[0]), 0, 8)
    keep_low, keep_high, ahead_low, ahead_high, back_low, back_high, far_low, far_high = parts
    half, mark = grad_head_half(rows, logit_grad, mark)
    ahead_low, _ = add(ahead_low, fetch(far_low, final(-1)), mark)
    back_high, mark = add(back_high, fetch(far_high, final(1)), mark)
    grad_head, mark = grad_head_half(rows, logit_grad, mark, half)
    parts = split_middle(
        (keep_low, fetch(ahead_low, final(-1)), fetch(back_low, final(1))),
        (keep_high, fetch(ahead_high, final(-1)), fetch(back_high, final(1))),
        mark,
    )
    parts = split_window(parts[0], *(fetch(parts[s], middle(-OFF[s])) for s in (1, 2, 3)))
    grad_hidden = finish(lax.all_to_all(parts, ("z", "c"), 0, 0, tiled=True))
    return grad_hidden, grad_head, loss[0, 0]


def solution(mesh):
    fine = Mesh(mesh.devices.reshape(NY, NX, NZ, NC), AXES)
    return jax.shard_map(
        local,
        mesh=fine,
        in_specs=(P(AXES, None), P(None, AXES), P(AXES), P(AXES), P(), P(), P()),
        out_specs=(P(AXES, None), P(None, AXES), P()),
        check_vma=False,
    )
```

```python
import functools

import jax
import jax.numpy as jnp
from jax import lax
from jax.experimental import pallas as pl
from jax.experimental.pallas import tpu as pltpu
from jax.sharding import Mesh, PartitionSpec as P

V = 163840
CODES = 32768
WIN = 48
NEG = -1e30
BETA = 1.0
LOSS_SCALE = 4096.0

D = 4096
HALF = D // 2
COLS = 640
TOKENS = 768
META = 128
WIDE = HALF + META
NY, NX, NZ, NC = 4, 4, 8, 2
AXES = ("y", "x", "z", "c")
OFF = (0, 1, 3, 2)
bf16 = jnp.bfloat16
f32 = jnp.float32
VMEM = pl.BlockSpec(memory_space=pltpu.VMEM)
SMEM = pl.BlockSpec(memory_space=pltpu.SMEM)
HBM = pl.BlockSpec(memory_space=pltpu.HBM)
MB = 1024 * 1024
PIECE = HALF // 2


def flat(y, x, z, c):
    return ((y % NY * NX + x % NX) * NZ + z % NZ) * NC + c


def fetch(value, source):
    pairs = [
        (flat(*source(y, x, z, c)), flat(y, x, z, c))
        for y in range(NY) for x in range(NX) for z in range(NZ) for c in range(NC)
    ]
    return lax.ppermute(value, AXES, pairs)


def middle(step):
    return lambda y, x, z, c: (y + step, x, z, c) if c == 0 else (y, x + step, z, c)


def final(step):
    return lambda y, x, z, c: (y, x + step, z, c) if c == 0 else (y + step, x, z, c)


def near(y, x, z, c):
    return y, x, z, 1 - c


def window(ids, core, s, k):
    y, x = ids[0], ids[1]
    across = core == 0
    last = (jnp.where(across, x, y) + OFF[s]) % 4
    mid = (jnp.where(across, y, x) + OFF[k]) % 4
    return jnp.where(across, mid * NX + last, last * NX + mid)


def call(kernel, outs, ins, scratch=(), vmem=10, **cost):
    return pl.pallas_call(
        kernel,
        out_shape=outs,
        in_specs=ins,
        out_specs=jax.tree.map(lambda _: VMEM, outs),
        scratch_shapes=list(scratch),
        compiler_params=pltpu.CompilerParams(vmem_limit_bytes=vmem * MB),
        cost_estimate=pl.CostEstimate(
            flops=cost.get("flops", 0), bytes_accessed=cost.get("bytes_accessed", 0), transcendentals=0
        ),
    )


def shape(dims, dtype):
    return jax.ShapeDtypeStruct(dims, dtype)


def first_message_kernel(targets, hidden, out, tok):
    rows = hidden[...].astype(f32)
    row = lax.broadcasted_iota(jnp.int32, (16, 128), 0)
    lane = lax.broadcasted_iota(jnp.int32, (16, 128), 1)
    meta = jnp.zeros((16, 128), f32)
    for j in range(3):
        goal = targets[j]
        for n, digit in enumerate((goal & 255, (goal >> 8) & 255, goal >> 16)):
            meta = jnp.where((row == j) & (lane == n), digit.astype(f32), meta)
    meta = meta.astype(bf16)
    for half in range(2):
        for r in range(16):
            at = half * HALF + r * 128
            tok[pl.ds(r, 3, stride=16), :] = rows[:, at:at + 128]
        part = tok[...].astype(bf16)
        for z in range(NZ):
            out[2 * z + half, 0:48, :] = part
            out[2 * z + half, 48:64, :] = meta


def first_message(targets, hidden):
    return call(
        first_message_kernel, shape((16, 64, 128), bf16), [SMEM, VMEM], [pltpu.VMEM((48, 128), f32)], vmem=56
    )(targets, hidden)


def join_window_kernel(ids, parts, out, tok, meta):
    for dev in range(16):
        tok[dev * 48:(dev + 1) * 48, :] = parts[dev, 0:48, :].astype(f32)
        meta[dev * 16:(dev + 1) * 16, :] = parts[dev, 48:64, :].astype(f32)
    for j in range(3):
        for r in range(16):
            out[j * 16:(j + 1) * 16, r * 128:(r + 1) * 128] = tok[pl.ds(j * 16 + r, 16, stride=48), :].astype(bf16)
        out[j * 16:(j + 1) * 16, HALF:WIDE] = meta[pl.ds(j, 16, stride=16), :].astype(bf16)


def join_window(ids, parts):
    return call(
        join_window_kernel,
        shape((WIN, WIDE), bf16),
        [SMEM, VMEM],
        [pltpu.VMEM((768, 128), f32), pltpu.VMEM((256, 128), f32)],
    )(ids, parts)


def all_arrived_kernel(a, b, c, mark):
    mark[...] = jnp.zeros_like(mark)


def all_arrived(*values):
    return call(all_arrived_kernel, shape((8, 128), f32), [VMEM] * 3)(*values)


def join_blocks_kernel(a, b, c, d, loaded, swapped, low, high):
    low[0], low[1], high[0], high[1] = a[...], b[...], c[...], d[...]


def join_blocks(*blocks):
    return call(join_blocks_kernel, [shape((2, WIN, WIDE), bf16)] * 2, [VMEM] * 6)(*blocks)


def columns_of(rows):
    full = jnp.concatenate([rows, jnp.zeros((128 - rows.shape[0], 128), f32)], axis=0)
    return full.T


def load_kernel(head_hbm, head, mark, sem):
    mark[...] = jnp.zeros_like(mark)
    copy = pltpu.make_async_copy(head_hbm, head, sem)
    copy.start()
    copy.wait()


def load_head(head):
    return call(
        load_kernel,
        (shape((D, COLS), bf16), shape((8, 128), f32)),
        [HBM],
        [pltpu.SemaphoreType.DMA],
        vmem=8,
        bytes_accessed=10 * MB,
    )(head)


def logits_kernel(
    ids, *refs
):
    own_blocks, other_blocks = refs[:8], refs[8:16]
    head, hidden, logits, stats, target, meta, cols = refs[16:]
    rows = 256
    core = ids[3]
    own = pl.multiple_of(core * HALF, HALF)
    oth = pl.multiple_of((1 - core) * HALF, HALF)
    for i, (a, b) in enumerate(zip(own_blocks, other_blocks)):
        for inner in range(2):
            s, k = i // 2, i % 2 * 2 + inner
            row = pl.multiple_of(window(ids, core, s, k) * WIN, 16)
            hidden[pl.ds(row, WIN), pl.ds(own, HALF)] = a[inner, :, 0:HALF]
            meta[pl.ds(row, WIN), :] = a[inner, :, HALF:WIDE].astype(f32)
            row = pl.multiple_of(window(ids, 1 - core, s, k) * WIN, 16)
            hidden[pl.ds(row, WIN), pl.ds(oth, HALF)] = b[inner, :, 0:HALF]
    first = ids[4] * COLS
    column = first + lax.broadcasted_iota(jnp.int32, (rows, COLS), 1)
    lane = lax.broadcasted_iota(jnp.int32, (rows, 128), 1)
    for i in range(TOKENS // rows):
        at = pl.ds(i * rows, rows)
        part = jnp.dot(hidden[at, :], head[...], preferred_element_type=f32)
        logits[at, :] = part
        digits = meta[at, :]
        goal = (digits[:, 0:1] + 256.0 * digits[:, 1:2] + 65536.0 * digits[:, 2:3]).astype(jnp.int32)
        in_range = (goal >= V - CODES) == (column >= V - CODES)
        masked = jnp.where(in_range, part, NEG)
        peak = jnp.max(masked, axis=1, keepdims=True)
        total = jnp.sum(jnp.where(in_range, jnp.exp(masked - peak), 0.0), axis=1, keepdims=True)
        hit = jnp.sum(jnp.where(column == goal, part, 0.0), axis=1, keepdims=True)
        norm = peak + jnp.log(jnp.maximum(total, 1e-37))
        cols[at, :] = jnp.where(lane == 0, norm, jnp.where(lane == 1, hit, goal.astype(f32)))
    stats[...] = jnp.zeros_like(stats)
    target[...] = jnp.zeros_like(target)
    for b in range(TOKENS // 128):
        turned = cols[b * 128:(b + 1) * 128, :].T
        for i in range(2):
            stats[i, b:b + 1, :] = turned[i:i + 1, :]
        target[b:b + 1, :] = turned[2:3, :]


def local_logits(ids, own, other, head):
    return pl.pallas_call(
        logits_kernel,
        out_shape=(
            shape((TOKENS, D), bf16),
            shape((TOKENS, COLS), f32),
            shape((2, 8, 128), f32),
            shape((8, 128), f32),
        ),
        in_specs=[SMEM] + [VMEM] * 17,
        out_specs=(VMEM, VMEM, VMEM, VMEM),
        scratch_shapes=[
            pltpu.VMEM((TOKENS, 128), f32),
            pltpu.VMEM((TOKENS, 128), f32),
        ],
        compiler_params=pltpu.CompilerParams(vmem_limit_bytes=25 * MB),
        cost_estimate=pl.CostEstimate(flops=2 * TOKENS * D * COLS, bytes_accessed=20 * MB, transcendentals=0),
    )(ids, *own, *other, head)


def exchange(value, axes):
    return lax.all_to_all(jnp.broadcast_to(value[None], (16,) + value.shape), axes, 0, 0, tiled=True)


def merged(parts):
    peak = parts[0, 0]
    for i in range(1, 16):
        peak = jnp.maximum(peak, parts[i, 0])
    total = jnp.zeros_like(peak)
    hit = jnp.zeros_like(peak)
    for i in range(16):
        total += jnp.exp(parts[i, 0] - peak)
        hit += parts[i, 1]
    return peak + jnp.log(total), hit


def merge_kernel(parts, out):
    norm, hit = merged(parts)
    for i in range(16):
        out[i, 0], out[i, 1] = norm, hit


def merge(parts):
    return call(merge_kernel, shape((16, 2, 8, 128), f32), [VMEM])(parts)


def preference_kernel(parts, lengths, ref_logps, pairing, norm, weight, loss):
    log_norm, hit = merged(parts)
    token_lp = hit - log_norm
    rows = lax.broadcasted_iota(jnp.int32, (8, 128), 0) * 128 + lax.broadcasted_iota(jnp.int32, (8, 128), 1)
    inner = rows % WIN
    group, position = rows // WIN, inner % 16 * 3 + inner // 16
    pairs = pairing.shape[0] // 2
    token_weight = jnp.zeros((8, 128), f32)
    losses = jnp.zeros((1, 1), f32)
    for k in range(pairs):
        sides = []
        for g in (pairing[2 * k], pairing[2 * k + 1]):
            count = lengths[g].astype(f32)
            live = (group == g) & (position < lengths[g])
            policy = jnp.sum(jnp.where(live, token_lp, 0.0), keepdims=True) / count
            sides.append((live, count, policy - ref_logps[g]))
        (live_c, count_c, chosen), (live_r, count_r, rejected) = sides
        margin = BETA * (chosen - rejected)
        losses += jnp.maximum(-margin, 0.0) + jnp.log1p(jnp.exp(-jnp.abs(margin)))
        pair_weight = -LOSS_SCALE * BETA * jax.nn.sigmoid(-margin) / pairs
        token_weight += jnp.where(live_c, pair_weight / count_c, 0.0)
        token_weight -= jnp.where(live_r, pair_weight / count_r, 0.0)
    norm[...] = log_norm
    weight[...] = token_weight
    loss[...] = jnp.broadcast_to(losses / pairs, (8, 128))


def preference(parts, lengths, ref_logps, pairing):
    return call(
        preference_kernel,
        [shape((8, 128), f32)] * 3,
        [VMEM, SMEM, SMEM, SMEM],
    )(parts, lengths, ref_logps, pairing)


BLOCK = 512
STEP = 256


def times_head(grad, rows):
    return lax.dot_general(grad, rows, (((1,), (1,)), ((), ())), preferred_element_type=f32)


def head_rows(half, start):
    return pl.ds(pl.multiple_of(half * HALF + start, STEP), STEP)


def other_piece(piece, ids, grad, head, out):
    for i in range(PIECE // STEP):
        rows = head[head_rows(1 - ids[3], piece * PIECE + i * STEP), :]
        out[:, i * STEP:(i + 1) * STEP] = times_head(grad[...], rows).astype(out.dtype)


def grad_other_first_kernel(ids, logits, norm, weight, target, head, grad, out):
    norm_c, weight_c, goal_c = columns_of(norm[...]), columns_of(weight[...]), columns_of(target[...])
    column = ids[4] * COLS + lax.broadcasted_iota(jnp.int32, (128, COLS), 1)
    for b in range(TOKENS // 128):
        goal = goal_c[:, b:b + 1].astype(jnp.int32)
        in_range = (goal >= V - CODES) == (column >= V - CODES)
        at = slice(b * 128, (b + 1) * 128)
        prob = jnp.exp(jnp.where(in_range, logits[at, :] - norm_c[:, b:b + 1], NEG))
        grad[at, :] = (weight_c[:, b:b + 1] * ((column == goal).astype(f32) - prob)).astype(bf16)
    other_piece(0, ids, grad, head, out)


def grad_other_first(ids, logits, norm, weight, target, head):
    return call(
        grad_other_first_kernel,
        (shape((TOKENS, COLS), bf16), shape((TOKENS, PIECE), bf16)),
        [SMEM] + [VMEM] * 5,
        vmem=16,
        flops=TOKENS * PIECE * COLS * 2,
        bytes_accessed=6 * MB,
    )(ids, logits, norm, weight, target, head)


def grad_other_second(ids, grad, head):
    return call(
        functools.partial(other_piece, 1),
        shape((TOKENS, PIECE), bf16),
        [SMEM, VMEM, VMEM],
        vmem=16,
        flops=TOKENS * PIECE * COLS * 4,
        bytes_accessed=16 * MB,
    )(ids, grad, head)


def arrived_kernel(value, mark):
    mark[...] = jnp.zeros_like(mark)


def arrived(value):
    return call(arrived_kernel, shape((8, 128), f32), [VMEM], vmem=4)(value)


def grad_own_kernel(ids, grad, head, out):
    for i in range(HALF // STEP):
        out[:, i * STEP:(i + 1) * STEP] = times_head(grad[...], head[head_rows(ids[3], i * STEP), :])


def grad_own(ids, grad, head):
    return call(
        grad_own_kernel,
        shape((TOKENS, HALF), f32),
        [SMEM, VMEM, VMEM],
        vmem=16,
        flops=TOKENS * HALF * COLS * 2,
        bytes_accessed=10 * MB,
    )(ids, grad, head)


PART_TYPES = (f32, f32, f32, bf16, bf16, f32, bf16, bf16)


def split_final_kernel(first, ids, own, other0, other1, after, *refs):
    parts, mark = refs[:-1], refs[-1]
    mark[...] = jnp.zeros_like(mark)
    for n, r in enumerate(parts, first):
        for inner in range(2):
            row = pl.multiple_of(window(ids, ids[3], n // 2, n % 2 * 2 + inner) * WIN, 16)
            for h, other in enumerate((other0, other1)):
                at = slice(h * PIECE, (h + 1) * PIECE)
                total = own[pl.ds(row, WIN), at] + other[pl.ds(row, WIN), :].astype(f32)
                r[inner, :, at] = total.astype(r.dtype)


def split_final(ids, own, other, after, first, last):
    return call(
        functools.partial(split_final_kernel, first),
        [shape((2, WIN, HALF), t) for t in PART_TYPES[first:last]] + [shape((8, 128), f32)],
        [SMEM] + [VMEM] * 4,
        vmem=18,
    )(ids, own, *other, after)


def head_kernel(hidden, grad, *refs):
    out, mark = refs[-2:]
    mark[...] = jnp.zeros_like(mark)
    out[...] = lax.dot_general(
        hidden[...], grad[...], (((0,), (0,)), ((), ())), preferred_element_type=f32
    ).astype(out.dtype)


def grad_head_half(hidden, grad, after, first=None):
    steps = D // BLOCK // 2
    base = 0 if first is None else steps
    return pl.pallas_call(
        head_kernel,
        grid=(steps,),
        in_specs=[
            pl.BlockSpec((TOKENS, BLOCK), lambda i: (0, i + base)),
            pl.BlockSpec((TOKENS, COLS), lambda i: (0, 0)),
            pl.BlockSpec((8, 128), lambda i: (0, 0)),
        ] + ([] if first is None else [pl.BlockSpec(memory_space=pl.ANY)]),
        out_specs=(pl.BlockSpec((BLOCK, COLS), lambda i: (i + base, 0)), pl.BlockSpec((8, 128), lambda i: (0, 0))),
        out_shape=(shape((D, COLS), bf16), shape((8, 128), f32)),
        input_output_aliases={} if first is None else {3: 0},
        compiler_params=pltpu.CompilerParams(vmem_limit_bytes=20 * MB),
        cost_estimate=pl.CostEstimate(flops=TOKENS * D * COLS, bytes_accessed=6 * MB, transcendentals=0),
    )(hidden, grad, after, *([] if first is None else [first]))


def add_four(a, b, c, d):
    return (a.astype(f32) + d.astype(f32)) + (b.astype(f32) + c.astype(f32))


def add_kernel(a, b, after, out, mark):
    mark[...] = jnp.zeros_like(mark)
    out[...] = (a[...] + b[...].astype(f32)).astype(out.dtype)


def add(a, b, after):
    return call(add_kernel, (shape(a.shape, bf16), shape((8, 128), f32)), [VMEM] * 3)(a, b, after)


def split_middle_kernel(*refs):
    ins, outs = refs[:6], refs[7:]
    for k, q in enumerate(outs):
        own, back, ahead = (ins[3 * (k // 2) + i][k % 2].astype(f32) for i in range(3))
        q[...] = (own + (back + ahead)).astype(q.dtype)


def split_middle(low, high, after):
    return call(
        split_middle_kernel,
        [shape((WIN, HALF), f32 if k == 0 else bf16) for k in range(4)],
        [VMEM] * 7,
        bytes_accessed=6 * MB,
    )(*low, *high, after)


def split_window_kernel(a, b, c, d, out, tok):
    total = add_four(a[...], b[...], c[...], d[...])
    for j in range(3):
        for r in range(16):
            tok[pl.ds(j * 16 + r, 16, stride=48), :] = total[j * 16:(j + 1) * 16, r * 128:(r + 1) * 128]
    for dev in range(16):
        out[dev] = tok[dev * 48:(dev + 1) * 48, :].astype(out.dtype)


def split_window(a, b, c, d):
    return call(
        split_window_kernel,
        shape((16, 48, 128), bf16),
        [VMEM] * 4,
        [pltpu.VMEM((768, 128), f32)],
    )(a, b, c, d)


def finish_kernel(parts, out, tok):
    for half in range(2):
        total = parts[half].astype(f32)
        for i in range(1, NZ):
            total += parts[2 * i + half].astype(f32)
        tok[...] = total
        for r in range(16):
            at = half * HALF + r * 128
            out[:, at:at + 128] = tok[pl.ds(r, 3, stride=16), :].astype(bf16)


def finish(parts):
    return call(finish_kernel, shape((3, D), bf16), [VMEM], [pltpu.VMEM((48, 128), f32)])(parts)


def local(hidden, head_weight, targets, image_mask, lengths, ref_logps, pairing):
    y, x, z, c = (lax.axis_index(a) for a in AXES)
    ids = jnp.stack([y, x, z, c, flat(y, x, z, c)]).astype(jnp.int32)

    parts = lax.all_to_all(first_message(targets, hidden), ("z", "c"), 0, 0, tiled=True)
    block = join_window(ids, parts)
    head, mark = load_head(head_weight)
    around = [fetch(block, middle(o)) for o in OFF[1:]]
    low, high = join_blocks(block, *around, mark, fetch(all_arrived(*around), near))
    ahead_low, back_high = fetch(low, final(1)), fetch(high, final(-1))
    ahead_high, back_low = fetch(high, final(1)), fetch(low, final(-1))
    far_low, far_high = fetch(ahead_low, final(1)), fetch(back_high, final(-1))
    own = [low, high, ahead_low, ahead_high, back_low, back_high, far_low, far_high]
    other = [fetch(v, near) for v in own]

    rows, logits, stats, target = local_logits(ids, own, other, head)
    stats = merge(exchange(stats, ("z", "c")))
    stats = lax.all_to_all(stats, ("y", "x"), 0, 0, tiled=True)
    log_norm, weight, loss = preference(stats, lengths, ref_logps, pairing)

    logit_grad, send = grad_other_first(ids, logits, log_norm, weight, target, head)
    received = [fetch(send, near)]
    received.append(fetch(grad_other_second(ids, logit_grad, head), near))
    own = grad_own(ids, logit_grad, head)
    *parts, mark = split_final(ids, own, received, arrived(received[0]), 0, 8)
    keep_low, keep_high, ahead_low, ahead_high, back_low, back_high, far_low, far_high = parts
    half, mark = grad_head_half(rows, logit_grad, mark)
    ahead_low, _ = add(ahead_low, fetch(far_low, final(-1)), mark)
    back_high, mark = add(back_high, fetch(far_high, final(1)), mark)
    grad_head, mark = grad_head_half(rows, logit_grad, mark, half)
    parts = split_middle(
        (keep_low, fetch(ahead_low, final(-1)), fetch(back_low, final(1))),
        (keep_high, fetch(ahead_high, final(-1)), fetch(back_high, final(1))),
        mark,
    )
    parts = split_window(parts[0], *(fetch(parts[s], middle(-OFF[s])) for s in (1, 2, 3)))
    grad_hidden = finish(lax.all_to_all(parts, ("z", "c"), 0, 0, tiled=True))
    return grad_hidden, grad_head, loss[0, 0]


def solution(mesh):
    fine = Mesh(mesh.devices.reshape(NY, NX, NZ, NC), AXES)
    return jax.shard_map(
        local,
        mesh=fine,
        in_specs=(P(AXES, None), P(None, AXES), P(AXES), P(AXES), P(), P(), P()),
        out_specs=(P(AXES, None), P(None, AXES), P()),
        check_vma=False,
    )
```
